256 devices in a mesh: section: 8 (over z), tile: 32 (over y, x, core).
Axes of the slice: x: 4, y: 4, z: 8, core: 2. Of those that a mesh axis runs over, the one named last changes fastest.
Arguments:
- frames_in: bfloat16 [8, 2, 32, 8, 60, 384], P('section', None, 'tile'), may hold values from -22 to 22
- cache: bfloat16 [8, 2, 32, 8, 60, 384], P('section', None, 'tile'), may hold values from -6 to 6
- kernel: bfloat16 [8, 3, 3, 3, 384, 384], P('section'), may hold values from -0.25 to 0.25
- gain: float32 [8, 384], P('section'), may hold values from 0.1 to 1.9
- conv_bias: float32 [8, 384], P('section'), may hold values from -3 to 3
Outputs:
- handed: bfloat16 [8, 2, 32, 8, 60, 384], P('section', None, 'tile')
- new_cache: bfloat16 [8, 2, 32, 8, 60, 384], P('section', None, 'tile')
The draws below stay inside these ranges and needn't reach their ends.
All inputs are finite; a program needn't handle non-finite values.
Results may differ from the reference program's by a relative error of at most 0.0031.
Values may be sent and summed in bfloat16 or wider, within the bound.
No kernel may reach another device: no remote copies, remote signals or barrier semaphores. Data moves between devices by JAX's collectives and lax.ppermute only.
A program may use at most 128 MiB of HBM per device.

```python
import jax
import jax.numpy as jnp
from jax import lax

C = 384
GROUPS = 32
FR = 2
W = 240
TCOL = 4
RD = 8
SECTIONS = 8
TILES = 32
TROW = 8
WD = 60
H = 64


def draw_frames_in(key, part):
    key = jax.random.fold_in(key, 7)
    keys = jax.random.split(key, 9)
    shape = (SECTIONS, FR, H, W, C)
    base = jnp.clip(jax.random.normal(keys[0], shape, jnp.float32), -3.5, 3.5)
    offset = jax.random.uniform(keys[1], (SECTIONS, FR, 1, 1, C), jnp.float32, 0.0, 2.0)
    rough_top = 3.0
    region_amp = 2.0
    rows = (jnp.arange(H, dtype=jnp.float32) / max(H - 1, 1))[None, None, :, None, None]
    cols = (jnp.arange(W, dtype=jnp.float32) / max(W - 1, 1))[None, None, None, :, None]
    upward = jax.random.randint(keys[2], (SECTIONS, FR, 1, 1, 1), 0, 2).astype(jnp.float32)
    height = upward * rows + (1.0 - upward) * (1.0 - rows)
    rise = jnp.exp(jnp.log(3.0) * height)
    rough = jnp.exp(jax.random.uniform(keys[3], (SECTIONS, 1, H, W, 1), jnp.float32, 0.0, jnp.log(rough_top)))
    chan = jnp.exp(jax.random.uniform(keys[4], (C,), jnp.float32, 0.0, jnp.log(2.0)))
    frame_scale = jnp.exp(jax.random.uniform(keys[5], (SECTIONS, FR, 1, 1, 1), jnp.float32, jnp.log(0.5), 0.0))
    coef = jax.random.uniform(keys[6], (2, SECTIONS, FR, 1, 1, 1), jnp.float32, 0.5, 1.0)
    turn = 2.0 * jax.random.randint(keys[7], (SECTIONS, FR, 1, 1, 1), 0, 2).astype(jnp.float32) - 1.0
    phase = jax.random.uniform(keys[8], (SECTIONS, FR, 1, 1, 1), jnp.float32, 0.0, 2.0)
    col_term = coef[0] * turn * (2.0 * cols - 1.0)
    row_term = coef[1] * jnp.cos(jnp.pi * (1.5 * rows + phase))
    region = region_amp * (col_term + row_term)
    values = 0.3 * (base * rise * rough * chan * frame_scale + offset + region)
    grid = values.reshape(SECTIONS, FR, TROW, RD, TCOL, WD, C).transpose(0, 1, 2, 4, 3, 5, 6)
    return grid.reshape(SECTIONS, FR, TILES, RD, WD, C).astype(jnp.bfloat16)


def block_levels(own_key, dims, cuts, least, largest):
    def one(dim, blocks):
        heights = jax.random.uniform(jax.random.fold_in(jax.random.fold_in(own_key, 6), dim), (blocks,), jnp.float32, least / len(cuts), largest / len(cuts))
        return jnp.repeat(jnp.exp(heights), dims[dim] // blocks).reshape((-1,) + (1,) * (len(dims) - dim - 1))

    loudness = one(*cuts[0])
    for cut in cuts[1:]:
        loudness = loudness * one(*cut)
    return loudness


def scatter_about(key, extent, scale, reach, pieces=(), held_as=jnp.bfloat16):
    level = block_levels(key, extent, pieces, -0.22, 0.18) if pieces else 1.0
    values = jax.random.normal(key, extent, jnp.float32) * scale * level
    return jnp.minimum(jnp.maximum(values, -reach), reach).astype(held_as)


def setup_inputs(seed: int = 0) -> dict:
    key_of = jax.random.split(jax.random.key(seed), 6)
    frames_in = draw_frames_in(jax.random.fold_in(key_of[5], 71), 0)
    cache = scatter_about(key_of[1], (SECTIONS, 2, TILES, RD, WD, C), 1.0, 6.0, ((0, 8), (2, 32)))
    kernel = scatter_about(key_of[2], (SECTIONS, 3, 3, 3, C, C), (27 * C // 16) ** -0.5, 0.25, ((0, 8),))
    gain = jnp.clip(1.0 + 0.18 * jax.random.normal(key_of[3], (SECTIONS, C), jnp.float32), 0.1, 1.9)
    conv_bias = scatter_about(key_of[4], (SECTIONS, C), 0.5, 3.0, ((0, 8),), jnp.float32)
    return {"frames_in": frames_in, "cache": cache, "kernel": kernel, "gain": gain, "conv_bias": conv_bias}


EPS = 1e-06

def to_image(tiled):
    frames = tiled.shape[0]
    grid = tiled.reshape(frames, TROW, TCOL, RD, WD, tiled.shape[-1])
    return grid.transpose(0, 1, 3, 2, 4, 5).reshape(frames, H, W, tiled.shape[-1])

def to_tiles(image):
    frames = image.shape[0]
    grid = image.reshape(frames, TROW, RD, TCOL, WD, image.shape[-1])
    return grid.transpose(0, 1, 3, 2, 4, 5).reshape(frames, TILES, RD, WD, image.shape[-1])

def convolve(padded, weights, frames, rows, width):
    chans = padded.shape[-1]
    total = jnp.zeros((frames * rows * width, weights.shape[-1]), jnp.float32)
    for step_t in range(3):
        for step_h in range(3):
            block = padded[step_t:step_t + frames, step_h:step_h + rows]
            taps = jnp.concatenate([block[:, :, step_w:step_w + width] for step_w in range(3)], axis=-1)
            taps = taps.reshape(-1, 3 * chans).astype(jnp.float32)
            matrix = weights[step_t, step_h].reshape(3 * chans, -1).astype(jnp.float32)
            total = total + jnp.dot(taps, matrix, precision=lax.Precision.HIGHEST)
    return total

def reference(frames_in, cache, kernel, gain, conv_bias):
    count = H * W * (C // GROUPS)
    outputs = []
    caches = []
    for section_id in range(SECTIONS):
        image_in = to_image(frames_in[section_id])
        image_cache = to_image(cache[section_id])
        values = image_in.astype(jnp.float32)
        grouped = values.reshape(FR, H, W, GROUPS, C // GROUPS)
        mean = lax.optimization_barrier(jnp.sum(grouped, axis=(1, 2, 4))) / count
        deviation = grouped - mean[:, None, None, :, None]
        var = lax.optimization_barrier(jnp.sum(deviation * deviation, axis=(1, 2, 4))) / count
        scaled = deviation * lax.rsqrt(var[:, None, None, :, None] + EPS)
        act = jax.nn.silu(scaled.reshape(FR, H, W, C) * gain[section_id]).astype(jnp.bfloat16)
        ext = jnp.concatenate([image_cache, act], axis=0)
        padded = jnp.pad(ext, ((0, 0), (1, 1), (1, 1), (0, 0)))
        total = convolve(padded, kernel[section_id], FR, H, W)
        result = values + conv_bias[section_id] + total.reshape(FR, H, W, C)
        outputs.append(to_tiles(result.astype(jnp.bfloat16)))
        caches.append(to_tiles(ext[-2:]))
    handed = jnp.stack([outputs[(section_id - 1) % SECTIONS] for section_id in range(SECTIONS)])
    return (handed, jnp.stack(caches))
```

```python
import functools

import jax
import jax.numpy as jnp
from jax import lax
from jax.experimental import pallas as pl
from jax.experimental.pallas import tpu as pltpu
from jax.sharding import PartitionSpec as P

GROUPS = 32
TCOL = 4
EPS = 1e-06
WP = 64
F32 = jnp.float32
BF16 = jnp.bfloat16
VMEM = pl.BlockSpec(memory_space=pltpu.VMEM)
ANY = pl.BlockSpec(memory_space=pl.ANY)
LIMIT = 20 * 1024 * 1024


def params():
    return pltpu.CompilerParams(vmem_limit_bytes=LIMIT)


def split3(x):
    high = x.astype(BF16)
    rest = x - high.astype(F32)
    mid = rest.astype(BF16)
    low = (rest - mid.astype(F32)).astype(BF16)
    return high, mid, low


def exact_dot(x, onehot):
    pad = jnp.zeros_like(x)
    parts = split3(x)
    lhs = jnp.concatenate([jnp.concatenate([p.astype(F32), pad], axis=0) for p in parts], axis=0)
    got = jnp.dot(lhs.astype(BF16), onehot, preferred_element_type=F32)
    return got[0:8] + got[16:24] + got[32:40]


def to_group(chans, block):
    size = chans // GROUPS
    chan = lax.broadcasted_iota(jnp.int32, (chans, 128), 0)
    lane = lax.broadcasted_iota(jnp.int32, (chans, 128), 1)
    first = (lane & (GROUPS - 1)) * size
    hit = (chan >= first) & (chan < first + size)
    if block is not None:
        hit = hit & ((lane >> 5) == block)
    return jnp.where(hit, 1.0, 0.0).astype(BF16)


def from_group(chans, block):
    size = chans // GROUPS
    lane = lax.broadcasted_iota(jnp.int32, (128, chans), 0)
    chan = lax.broadcasted_iota(jnp.int32, (128, chans), 1)
    first = (lane & (GROUPS - 1)) * size
    hit = (chan >= first) & (chan < first + size) & ((lane >> 5) == block)
    return jnp.where(hit, 1.0, 0.0).astype(BF16)


def first_kernel(x_ref, c_ref, stat_ref, send_a_ref, send_b_ref, left_scr, right_scr):
    frames, rows, width, chans = x_ref.shape
    size = chans // GROUPS
    count = rows * width
    odd = (lax.axis_index("tile") & 1) == 1
    for k in range(4):
        src = c_ref if k < 2 else x_ref
        for r in range(rows):
            left_scr[k * rows + r : k * rows + r + 1, :] = src[k % 2, r, 0:1, :].astype(F32)
            right_scr[k * rows + r : k * rows + r + 1, :] = src[k % 2, r, width - 1 : width, :].astype(F32)
    left, right = left_scr[...], right_scr[...]
    send_a_ref[...] = jnp.where(odd, left, right).astype(BF16)
    send_b_ref[...] = jnp.where(odd, right, left).astype(BF16)
    sums, squares = [], []
    for f in range(frames):
        x = x_ref[f].astype(F32)
        total = jnp.sum(jnp.sum(x, axis=0), axis=0, keepdims=True)
        dev = x - (total * (1.0 / count))[None]
        sums.append(total)
        squares.append(jnp.sum(jnp.sum(dev * dev, axis=0), axis=0, keepdims=True))
    zero = jnp.zeros((1, chans), F32)
    both = jnp.concatenate(sums + [zero] * 6, axis=0)
    grouped = exact_dot(both, to_group(chans, 0))
    spread = exact_dot(grouped, from_group(chans, 0))
    off = both * (1.0 / count) - spread * (1.0 / (count * size))
    square = jnp.concatenate(squares + [zero] * 6, axis=0) + count * off * off
    row = lax.broadcasted_iota(jnp.int32, (8, 128), 0)
    lane = lax.broadcasted_iota(jnp.int32, (8, 128), 1)
    every = to_group(chans, None)
    mix_sum = exact_dot(both, every)
    mix_square = exact_dot(square, every)
    kind = lane >> 5
    mixed = jnp.where((row == 0) & (kind == 0), mix_sum, 0.0)
    mixed = mixed + jnp.where((row == 1) & (kind == 2), mix_sum, 0.0)
    mixed = mixed + jnp.where((row == 0) & (kind == 1), mix_square, 0.0)
    mixed = mixed + jnp.where((row == 1) & (kind == 3), mix_square, 0.0)
    line = jnp.sum(mixed, axis=0, keepdims=True)
    stat_ref[...] = jnp.broadcast_to(line[None], stat_ref.shape)


def build_taps(frame, left, right, pad_ref, out_ref, rows):
    width, chans = frame.shape[1], frame.shape[2]
    pad_ref[:rows, 8 : 8 + width, :] = frame
    for r in range(rows):
        pad_ref[r, 7:8, :] = left[r : r + 1]
        pad_ref[r, 8 + width : 9 + width, :] = right[r : r + 1]
    for b in range(3):
        out_ref[:rows, :, b * chans : (b + 1) * chans] = pad_ref[:rows, 7 + b : 7 + b + WP, :].astype(BF16)


def cache_kernel(c_ref, x_ref, recv_a_ref, recv_b_ref, w_ref,
                 v_ref, x0_ref, x1_ref, acc0_ref, acc1_ref, top_ref, bottom_ref, left_ref, right_ref,
                 pad_ref, row_scr, sems):
    _, rows, width, chans = c_ref.shape
    copies = {}
    for a in range(3):
        for t in (0, 1):
            copies[t, a] = pltpu.make_async_copy(
                w_ref.at[t, a], v_ref.at[a, :, (2 - t) * chans : (3 - t) * chans], sems.at[t, a])
            copies[t, a].start()
    for a in range(3):
        copies[2, a] = pltpu.make_async_copy(w_ref.at[2, a], v_ref.at[a, :, 0:chans], sems.at[2, a])
        copies[2, a].start()
    odd = (lax.axis_index("tile") & 1) == 1
    got_a, got_b = recv_a_ref[...].astype(F32), recv_b_ref[...].astype(F32)
    left_ref[...] = jnp.where(odd, got_a, got_b)
    right_ref[...] = jnp.where(odd, got_b, got_a)
    pad_ref[...] = jnp.zeros_like(pad_ref)
    for k, out_ref in ((0, x0_ref), (1, x1_ref)):
        build_taps(c_ref[k].astype(F32), left_ref[k * rows : (k + 1) * rows], right_ref[k * rows : (k + 1) * rows],
                   pad_ref, out_ref, rows)
    for out_ref, r in ((top_ref, 0), (bottom_ref, rows - 1)):
        for k in range(4):
            src = c_ref if k < 2 else x_ref
            row_scr[...] = jnp.zeros_like(row_scr)
            row_scr[0:width, :] = src[k % 2, r].astype(F32)
            row_scr[width : width + 1, :] = left_ref[k * rows + r : k * rows + r + 1]
            row_scr[width + 1 : width + 2, :] = right_ref[k * rows + r : k * rows + r + 1]
            out_ref[k] = row_scr[...].astype(BF16)
    inner = rows - 2
    acc0 = jnp.zeros((inner * WP, chans), F32)
    acc1 = jnp.zeros((inner * WP, chans), F32)
    for a in range(3):
        copies[0, a].wait()
        copies[1, a].wait()
        lhs0 = x0_ref[a : a + inner].reshape(inner * WP, 3 * chans)
        lhs1 = x1_ref[a : a + inner].reshape(inner * WP, 3 * chans)
        acc0 = acc0 + jnp.dot(lhs0, v_ref[a, :, 2 * chans : 3 * chans], preferred_element_type=F32)
        part = jnp.dot(lhs1, v_ref[a, :, chans : 3 * chans], preferred_element_type=F32)
        acc0 = acc0 + part[:, :chans]
        acc1 = acc1 + part[:, chans:]
    acc0_ref[...] = acc0
    acc1_ref[...] = acc1
    for a in range(3):
        copies[2, a].wait()


def tile_place():
    tile = lax.axis_index("tile")
    return lax.div(tile, TCOL), lax.rem(tile, TCOL)


def silu(v):
    return v / (1.0 + jnp.exp(-v))


def activated(x, scale, shift):
    return silu(x * scale + shift)


def frame_taps(f, x_ref, left_ref, right_ref, scale, shift, pad_ref, out_ref):
    rows = x_ref.shape[1]
    _, col = tile_place()
    act = activated(x_ref[f].astype(F32), scale[None], shift[None])
    span = slice((2 + f) * rows, (3 + f) * rows)
    left = activated(left_ref[span], scale, shift)
    right = activated(right_ref[span], scale, shift)
    left = jnp.where(col > 0, left, 0.0)
    right = jnp.where(col < TCOL - 1, right, 0.0)
    pad_ref[...] = jnp.zeros_like(pad_ref)
    build_taps(act, left, right, pad_ref, out_ref, rows)


def finish_rows(total, x, bias, rows, width):
    chans = total.shape[-1]
    return (x.astype(F32) + bias[None] + total.reshape(rows, WP, chans)[:, :width]).astype(BF16)


def frame0_kernel(tiles, stat_ref, x_ref, left_ref, right_ref, v_ref, acc0_ref, gain_ref, bias_ref,
                  y_ref, coef_ref, xa_ref, pad_ref):
    _, rows, width, chans = x_ref.shape
    part = rows * width * (chans // GROUPS)
    count = part * tiles
    stat = stat_ref[...].reshape(tiles, 128)
    moved = pltpu.roll(stat, GROUPS, 1)
    mean = jnp.sum(stat, axis=0, keepdims=True) * (1.0 / count)
    mean_moved = jnp.sum(moved, axis=0, keepdims=True) * (1.0 / count)
    off = moved * (1.0 / part) - mean_moved
    var = jnp.sum(stat + part * off * off, axis=0, keepdims=True) * (1.0 / count)
    lane = lax.broadcasted_iota(jnp.int32, (1, 128), 1)
    is_mean = ((lane >> 5) & 1) == 0
    both = jnp.where(is_mean, mean, lax.rsqrt(jnp.maximum(var, 0.0) + EPS))
    both = jnp.broadcast_to(both, (8, 128))
    gain = gain_ref[...]
    for f in range(2):
        means = exact_dot(both, from_group(chans, 2 * f))[0:1]
        rstds = exact_dot(both, from_group(chans, 2 * f + 1))[0:1]
        scale = rstds * gain
        coef_ref[2 * f : 2 * f + 1, :] = scale
        coef_ref[2 * f + 1 : 2 * f + 2, :] = -means * scale
    frame_taps(0, x_ref, left_ref, right_ref, coef_ref[0:1], coef_ref[1:2], pad_ref, xa_ref)
    inner = rows - 2
    total = acc0_ref[...]
    for a in range(3):
        lhs = xa_ref[a : a + inner].reshape(inner * WP, 3 * chans)
        total = total + jnp.dot(lhs, v_ref[a, :, 0:chans], preferred_element_type=F32)
    y_ref[...] = finish_rows(total, x_ref[0, 1 : rows - 1], bias_ref[...], inner, width)


def frame1_kernel(x_ref, left_ref, right_ref, v_ref, acc1_ref, coef_ref, bias_ref, xa0_ref,
                  y_ref, xa_ref, pad_ref):
    _, rows, width, chans = x_ref.shape
    frame_taps(1, x_ref, left_ref, right_ref, coef_ref[2:3], coef_ref[3:4], pad_ref, xa_ref)
    inner = rows - 2
    total = acc1_ref[...]
    for a in range(3):
        lhs = xa0_ref[a : a + inner].reshape(inner * WP, 3 * chans)
        total = total + jnp.dot(lhs, v_ref[a, :, chans : 2 * chans], preferred_element_type=F32)
        lhs = xa_ref[a : a + inner].reshape(inner * WP, 3 * chans)
        total = total + jnp.dot(lhs, v_ref[a, :, 0:chans], preferred_element_type=F32)
    y_ref[...] = finish_rows(total, x_ref[1, 1 : rows - 1], bias_ref[...], inner, width)


def edge_kernel(x_ref, above_ref, below_ref, v_ref, coef_ref, bias_ref, x0_ref, x1_ref, xa0_ref, xa1_ref,
                y_ref, new_ref, pad_ref, halo_ref):
    _, rows, width, chans = x_ref.shape
    row, col = tile_place()
    last = lax.div(lax.axis_size("tile"), TCOL) - 1
    pad_ref[...] = jnp.zeros_like(pad_ref)
    total0 = jnp.zeros((2 * WP, chans), F32)
    total1 = jnp.zeros((2 * WP, chans), F32)
    for k, taps_ref in enumerate((x0_ref, x1_ref, xa0_ref, xa1_ref)):
        for side, src in ((0, above_ref), (1, below_ref)):
            cells = src[k].astype(F32)
            if k >= 2:
                f = k - 2
                cells = activated(cells, coef_ref[2 * f : 2 * f + 1], coef_ref[2 * f + 1 : 2 * f + 2])
                at = lax.broadcasted_iota(jnp.int32, cells.shape, 0)
                inside = (row > 0) if side == 0 else (row < last)
                keep = (at < width) | ((at == width) & (col > 0)) | ((at == width + 1) & (col < TCOL - 1))
                cells = jnp.where(keep & inside, cells, 0.0)
            pad_ref[side, 8 : 8 + width, :] = cells[0:width]
            pad_ref[side, 7:8, :] = cells[width : width + 1]
            pad_ref[side, 8 + width : 9 + width, :] = cells[width + 1 : width + 2]
        for b in range(3):
            halo_ref[:, :, b * chans : (b + 1) * chans] = pad_ref[0:2, 7 + b : 7 + b + WP, :].astype(BF16)
        lo, hi = ((2, 3), (1, 3), (0, 2), (0, 1))[k]
        for a in range(3):
            up = halo_ref[0] if a == 0 else taps_ref[a - 1]
            down = halo_ref[1] if a == 2 else taps_ref[rows - 2 + a]
            lhs = jnp.concatenate([up, down], axis=0)
            part = jnp.dot(lhs, v_ref[a, :, lo * chans : hi * chans], preferred_element_type=F32)
            if k == 0:
                total0 = total0 + part
            elif k == 3:
                total1 = total1 + part
            else:
                total0 = total0 + part[:, :chans]
                total1 = total1 + part[:, chans:]
    for f, total in ((0, total0), (1, total1)):
        for side, r in ((0, 0), (1, rows - 1)):
            y_ref[f, side] = (x_ref[f, r].astype(F32) + bias_ref[...]
                              + total[side * WP : side * WP + width]).astype(BF16)
    new_ref[0] = xa0_ref[:, 0:width, chans : 2 * chans]
    new_ref[1] = xa1_ref[:, 0:width, chans : 2 * chans]


def join_kernel(y0_ref, y1_ref, edge_ref, out_ref, sems):
    rows = out_ref.shape[1]
    copies = []
    for f, src in ((0, y0_ref), (1, y1_ref)):
        copies.append(pltpu.make_async_copy(src, out_ref.at[f, 1 : rows - 1], sems.at[f, 0]))
        copies.append(pltpu.make_async_copy(edge_ref.at[f, 0], out_ref.at[f, 0], sems.at[f, 1]))
        copies.append(pltpu.make_async_copy(edge_ref.at[f, 1], out_ref.at[f, rows - 1], sems.at[f, 2]))
    for copy in copies:
        copy.start()
    for copy in copies:
        copy.wait()


def on_device(frames_in, cache, kernel, gain, conv_bias):
    x = frames_in[0][:, 0]
    c = cache[0][:, 0]
    frames, rows, width, chans = x.shape
    tiles = lax.axis_size("tile")
    sections = lax.axis_size("section")
    weights = kernel.reshape(3, 3, 3 * chans, chans)
    inner = rows - 2
    sds = jax.ShapeDtypeStruct

    stat, send_a, send_b = pl.pallas_call(
        first_kernel,
        out_shape=(sds((tiles, 1, 128), F32), sds((4 * rows, chans), BF16), sds((4 * rows, chans), BF16)),
        in_specs=[VMEM] * 2, out_specs=[VMEM] * 3,
        scratch_shapes=[pltpu.VMEM((4 * rows, chans), F32)] * 2,
        compiler_params=params(), name="local_stats",
    )(x, c)
    swap_a = [(i, i ^ 1) for i in range(tiles)]
    swap_b = [(i, i + (1 if i % 2 else -1)) for i in range(tiles) if i % TCOL in (1, 2)]
    recv_a = lax.ppermute(send_a, "tile", swap_a)
    recv_b = lax.ppermute(send_b, "tile", swap_b)
    stats = lax.all_to_all(stat, "tile", 0, 0, tiled=True)

    taps = pltpu.VMEM((rows, WP, 3 * chans), BF16)
    acc = pltpu.VMEM((inner * WP, chans), F32)
    cols = pltpu.VMEM((4 * rows, chans), F32)
    v, x0, x1, acc0, acc1, top, bottom, left, right = pl.pallas_call(
        cache_kernel,
        out_shape=(pltpu.VMEM((3, 3 * chans, 3 * chans), BF16), taps, taps, acc, acc,
                   sds((4, WP, chans), BF16), sds((4, WP, chans), BF16), cols, cols),
        in_specs=[VMEM] * 4 + [ANY], out_specs=[VMEM] * 9,
        scratch_shapes=[pltpu.VMEM((rows, 80, chans), F32), pltpu.VMEM((WP, chans), F32),
                        pltpu.SemaphoreType.DMA((3, 3))],
        compiler_params=params(), name="cache_part",
    )(c, x, recv_a, recv_b, weights)
    above = lax.ppermute(bottom, "tile", [(i, i + TCOL) for i in range(tiles - TCOL)])
    below = lax.ppermute(top, "tile", [(i + TCOL, i) for i in range(tiles - TCOL)])

    onward = [(i, (i + 1) % sections) for i in range(sections)]
    y0, coef, xa0 = pl.pallas_call(
        functools.partial(frame0_kernel, tiles),
        out_shape=(sds((inner, width, chans), BF16), pltpu.VMEM((8, chans), F32), taps),
        in_specs=[VMEM] * 8, out_specs=[VMEM] * 3,
        scratch_shapes=[pltpu.VMEM((rows, 80, chans), F32)],
        compiler_params=params(), name="frame0_inner",
    )(stats, x, left, right, v, acc0, gain, conv_bias)
    y0 = lax.ppermute(y0, "section", onward)
    y1, xa1 = pl.pallas_call(
        frame1_kernel,
        out_shape=(sds((inner, width, chans), BF16), taps),
        in_specs=[VMEM] * 8, out_specs=[VMEM] * 2,
        scratch_shapes=[pltpu.VMEM((rows, 80, chans), F32)],
        compiler_params=params(), name="frame1_inner",
    )(x, left, right, v, acc1, coef, conv_bias, xa0)
    y1 = lax.ppermute(y1, "section", onward)
    edge, new = pl.pallas_call(
        edge_kernel,
        out_shape=(sds((2, 2, width, chans), BF16), sds((frames, rows, width, chans), BF16)),
        in_specs=[VMEM] * 10, out_specs=[VMEM] * 2,
        scratch_shapes=[pltpu.VMEM((2, 80, chans), F32), pltpu.VMEM((2, WP, 3 * chans), BF16)],
        compiler_params=params(), name="edge_rows",
    )(x, above, below, v, coef, conv_bias, x0, x1, xa0, xa1)
    edge = lax.ppermute(edge, "section", onward)
    handed = pl.pallas_call(
        join_kernel,
        out_shape=sds((frames, rows, width, chans), BF16),
        in_specs=[ANY] * 3, out_specs=ANY,
        scratch_shapes=[pltpu.SemaphoreType.DMA((2, 3))],
        compiler_params=params(), name="join_rows",
    )(y0, y1, edge)
    return (handed[None, :, None], new[None, :, None])


def solution(mesh):
    tiled = P("section", None, "tile", None, None, None)
    in_specs = (tiled, tiled, P("section", None, None, None, None, None), P("section", None), P("section", None))
    return jax.shard_map(
        on_device, mesh=mesh, in_specs=in_specs, out_specs=(tiled, tiled), check_vma=False
    )
```

```python
import functools

import jax
import jax.numpy as jnp
from jax import lax
from jax.experimental import pallas as pl
from jax.experimental.pallas import tpu as pltpu
from jax.sharding import PartitionSpec as P

GROUPS = 32
TCOL = 4
EPS = 1e-06
WP = 64
F32 = jnp.float32
BF16 = jnp.bfloat16
VMEM = pl.BlockSpec(memory_space=pltpu.VMEM)
ANY = pl.BlockSpec(memory_space=pl.ANY)
LIMIT = 20 * 1024 * 1024


def cost(us):
    return pl.CostEstimate(flops=int(us * 1e9), bytes_accessed=int(us * 3e6), transcendentals=0)


def params():
    return pltpu.CompilerParams(vmem_limit_bytes=LIMIT)


def split3(x):
    high = x.astype(BF16)
    rest = x - high.astype(F32)
    mid = rest.astype(BF16)
    low = (rest - mid.astype(F32)).astype(BF16)
    return high, mid, low


def exact_dot(x, onehot):
    pad = jnp.zeros_like(x)
    parts = split3(x)
    lhs = jnp.concatenate([jnp.concatenate([p.astype(F32), pad], axis=0) for p in parts], axis=0)
    got = jnp.dot(lhs.astype(BF16), onehot, preferred_element_type=F32)
    return got[0:8] + got[16:24] + got[32:40]


def to_group(chans, block):
    size = chans // GROUPS
    chan = lax.broadcasted_iota(jnp.int32, (chans, 128), 0)
    lane = lax.broadcasted_iota(jnp.int32, (chans, 128), 1)
    first = (lane & (GROUPS - 1)) * size
    hit = (chan >= first) & (chan < first + size)
    if block is not None:
        hit = hit & ((lane >> 5) == block)
    return jnp.where(hit, 1.0, 0.0).astype(BF16)


def from_group(chans, block):
    size = chans // GROUPS
    lane = lax.broadcasted_iota(jnp.int32, (128, chans), 0)
    chan = lax.broadcasted_iota(jnp.int32, (128, chans), 1)
    first = (lane & (GROUPS - 1)) * size
    hit = (chan >= first) & (chan < first + size) & ((lane >> 5) == block)
    return jnp.where(hit, 1.0, 0.0).astype(BF16)


PARTS = 4


def fetch(hbm_ref, f, vmem_ref, sems):
    step = hbm_ref.shape[1] // PARTS
    copies = [pltpu.make_async_copy(hbm_ref.at[f, pl.ds(p * step, step)], vmem_ref.at[pl.ds(p * step, step)],
                                    sems.at[p]) for p in range(PARTS)]
    for copy in copies:
        copy.start()
    return copies


def wait_all(copies):
    for copy in copies:
        copy.wait()


def first_kernel(x_hbm, c_hbm, stat_ref, first_ref, last_ref, x_ref, edge_ref, sems, edge_sems):
    frames, width, rows, chans = x_ref.shape
    loads = [fetch(x_hbm, f, x_ref.at[f], sems.at[f]) for f in range(frames)]
    edges = []
    for f in range(2):
        for at, w in ((0, 0), (1, width - 1)):
            edges.append(pltpu.make_async_copy(c_hbm.at[f, w], edge_ref.at[f, at], edge_sems.at[f, at]))
    for copy in edges:
        copy.start()
    size = chans // GROUPS
    count = rows * width
    sums, squares = [], []
    for f in range(frames):
        wait_all(loads[f])
        x = x_ref[f].astype(F32)
        total = jnp.sum(jnp.sum(x, axis=0), axis=0, keepdims=True)
        dev = x - (total * (1.0 / count))[None]
        sums.append(total)
        squares.append(jnp.sum(jnp.sum(dev * dev, axis=0), axis=0, keepdims=True))
    wait_all(edges)
    for k in range(4):
        first_ref[k] = edge_ref[k, 0] if k < 2 else x_ref[k - 2, 0]
        last_ref[k] = edge_ref[k, 1] if k < 2 else x_ref[k - 2, width - 1]
    zero = jnp.zeros((1, chans), F32)
    both = jnp.concatenate(sums + [zero] * 6, axis=0)
    grouped = exact_dot(both, to_group(chans, 0))
    spread = exact_dot(grouped, from_group(chans, 0))
    off = both * (1.0 / count) - spread * (1.0 / (count * size))
    square = jnp.concatenate(squares + [zero] * 6, axis=0) + count * off * off
    row = lax.broadcasted_iota(jnp.int32, (8, 128), 0)
    lane = lax.broadcasted_iota(jnp.int32, (8, 128), 1)
    every = to_group(chans, None)
    mix_sum = exact_dot(both, every)
    mix_square = exact_dot(square, every)
    kind = lane >> 5
    mixed = jnp.where((row == 0) & (kind == 0), mix_sum, 0.0)
    mixed = mixed + jnp.where((row == 1) & (kind == 2), mix_sum, 0.0)
    mixed = mixed + jnp.where((row == 0) & (kind == 1), mix_square, 0.0)
    mixed = mixed + jnp.where((row == 1) & (kind == 3), mix_square, 0.0)
    line = jnp.sum(mixed, axis=0, keepdims=True)
    stat_ref[...] = jnp.broadcast_to(line[None], stat_ref.shape)


LANES = 128


def put_lines(flat_ref, lines):
    for j in range(flat_ref.shape[0]):
        flat_ref[j] = lines[:, j * LANES : (j + 1) * LANES]


def get_row(flat_ref, r, rows, width):
    return jnp.concatenate(
        [flat_ref[j, pl.ds(r, width, stride=rows), :] for j in range(flat_ref.shape[0])], axis=1)


def put_row(flat_ref, r, rows, width, value):
    for j in range(flat_ref.shape[0]):
        flat_ref[j, pl.ds(r, width, stride=rows), :] = value[:, j * LANES : (j + 1) * LANES]


def build_taps(flat_ref, left, right, pad_ref, out_ref, rows, width):
    chans = pad_ref.shape[-1]
    for r in range(rows):
        pad_ref[r, 8 : 8 + width, :] = get_row(flat_ref, r, rows, width)
        pad_ref[r, 7:8, :] = left[r : r + 1]
        pad_ref[r, 8 + width : 9 + width, :] = right[r : r + 1]
    for b in range(3):
        out_ref[1 : 1 + rows, :, b * chans : (b + 1) * chans] = pad_ref[:, 7 + b : 7 + b + WP, :].astype(BF16)
    out_ref[0] = jnp.zeros_like(out_ref[0])
    out_ref[rows + 1] = jnp.zeros_like(out_ref[0])


def clear_tail(pad_ref, width):
    pad_ref[:, 8 + width :, :] = jnp.zeros_like(pad_ref[:, 8 + width :, :])


def tile_place():
    tile = lax.axis_index("tile")
    return lax.div(tile, TCOL), lax.rem(tile, TCOL)


BLOCK = 4


def wide_taps(taps_ref, first):
    return jnp.concatenate([taps_ref[first + a : first + a + BLOCK].reshape(BLOCK * WP, -1) for a in range(3)], axis=1)


def product(taps_ref, first, v_ref, at):
    return jnp.dot(wide_taps(taps_ref, first), tap_weights(v_ref, at, at + 1), preferred_element_type=F32)


def tap_weights(v_ref, lo, hi):
    chans = v_ref.shape[1] // 3
    return v_ref[:, :, lo * chans : hi * chans].reshape(9 * chans, (hi - lo) * chans)


def rows_kernel(c_hbm, x_hbm, from_left_ref, from_right_ref, bottom_ref, top_ref, left_ref, right_ref,
                frame_ref, flat_ref, sems):
    _, width, rows, chans = frame_ref.shape
    loads = [fetch(c_hbm if k < 2 else x_hbm, k % 2, frame_ref.at[k], sems.at[k]) for k in range(4)]
    _, col = tile_place()
    left_ref[...] = jnp.where(col > 0, from_left_ref[...].astype(F32), 0.0)
    right_ref[...] = jnp.where(col < TCOL - 1, from_right_ref[...].astype(F32), 0.0)
    for k in range(4):
        wait_all(loads[k])
        put_lines(flat_ref, frame_ref[k].astype(F32).reshape(width * rows, chans))
        for out_ref, r in ((bottom_ref, rows - 1), (top_ref, 0)):
            last = jnp.concatenate([left_ref[k, r : r + 1], right_ref[k, r : r + 1],
                                    jnp.zeros((WP - width - 2, chans), F32)], axis=0)
            line = jnp.concatenate([get_row(flat_ref, r, rows, width), last], axis=0)
            out_ref[k] = line.astype(BF16)


def silu(v):
    return v / (1.0 + jnp.exp(-v))


def activated(x, scale, shift):
    return silu(x * scale + shift)


def frame_taps(f, x_ref, left_ref, right_ref, scale, shift, pad_ref, flat_ref, new_ref, out_ref):
    _, width, rows, chans = x_ref.shape
    _, col = tile_place()
    act = activated(x_ref[f].astype(F32).reshape(width * rows, chans), scale, shift)
    put_lines(flat_ref, act)
    new_ref[...] = act.astype(BF16).reshape(width, rows, chans)
    left = activated(left_ref[2 + f], scale, shift)
    right = activated(right_ref[2 + f], scale, shift)
    left = jnp.where(col > 0, left, 0.0)
    right = jnp.where(col < TCOL - 1, right, 0.0)
    clear_tail(pad_ref, width)
    build_taps(flat_ref, left, right, pad_ref, out_ref, rows, width)


def finish_rows(total, first, flat_ref, bias, width, rows, y_ref, rim_ref, skip=0):
    for at in range(BLOCK):
        r = first + at
        whole = get_row(flat_ref, r, rows, width) + bias + total[at * WP : at * WP + width]
        if r in (0, rows - 1):
            rim_ref[r // (rows - 1)] = whole
        else:
            y_ref[r - 1 - skip] = whole.astype(BF16)


def frame0_kernel(tiles, stat_ref, c_hbm, x_hbm, left_ref, right_ref, w_hbm, gain_ref, bias_ref,
                  y_ref, rim_ref, new_ref, v_ref, coef_ref, x_ref, x1_ref, xa_ref,
                  c_ref, x0_ref, sum_ref, pad_ref, flat_ref, frame_sems, sems):
    _, width, rows, chans = x_ref.shape
    copies = {}

    def load_weights(t):
        for a in range(3):
            copies[t, a] = pltpu.make_async_copy(
                w_hbm.at[t, a], v_ref.at[a, :, (2 - t) * chans : (3 - t) * chans], sems.at[t, a])
            copies[t, a].start()

    def wait_weights(t):
        for a in range(3):
            copies[t, a].wait()

    loads = [fetch(x_hbm, 0, x_ref.at[0], frame_sems.at[0]), fetch(c_hbm, 0, c_ref.at[0], frame_sems.at[1])]
    load_weights(0)
    loads.append(fetch(c_hbm, 1, c_ref.at[1], frame_sems.at[2]))
    load_weights(1)
    load_weights(2)
    loads.append(fetch(x_hbm, 1, x_ref.at[1], frame_sems.at[3]))
    firsts = range(0, rows, BLOCK)

    def cached_taps(k, out_ref):
        wait_all(loads[k + 1])
        put_lines(flat_ref, c_ref[k].astype(F32).reshape(width * rows, chans))
        build_taps(flat_ref, left_ref[k], right_ref[k], pad_ref, out_ref, rows, width)

    clear_tail(pad_ref, width)
    cached_taps(0, x0_ref)
    wait_all(loads[0])
    wait_weights(0)
    for first in firsts:
        sum_ref[first * WP : (first + BLOCK) * WP] = product(x0_ref, first, v_ref, 2)
    part = rows * width * (chans // GROUPS)
    count = part * tiles
    stat = stat_ref[...].reshape(tiles, 128)
    moved = pltpu.roll(stat, GROUPS, 1)
    mean = jnp.sum(stat, axis=0, keepdims=True) * (1.0 / count)
    mean_moved = jnp.sum(moved, axis=0, keepdims=True) * (1.0 / count)
    off = moved * (1.0 / part) - mean_moved
    var = jnp.sum(stat + part * off * off, axis=0, keepdims=True) * (1.0 / count)
    lane = lax.broadcasted_iota(jnp.int32, (1, 128), 1)
    is_mean = ((lane >> 5) & 1) == 0
    both = jnp.where(is_mean, mean, lax.rsqrt(jnp.maximum(var, 0.0) + EPS))
    both = jnp.broadcast_to(both, (8, 128))
    gain = gain_ref[...]
    for f in range(2):
        means = exact_dot(both, from_group(chans, 2 * f))[0:1]
        rstds = exact_dot(both, from_group(chans, 2 * f + 1))[0:1]
        scale = rstds * gain
        coef_ref[2 * f : 2 * f + 1, :] = scale
        coef_ref[2 * f + 1 : 2 * f + 2, :] = -means * scale
    frame_taps(0, x_ref, left_ref, right_ref, coef_ref[0:1], coef_ref[1:2], pad_ref, flat_ref, new_ref, xa_ref)
    cached_taps(1, x1_ref)
    wait_weights(1)
    for first in firsts:
        sum_ref[first * WP : (first + BLOCK) * WP] += product(x1_ref, first, v_ref, 1)
    put_lines(flat_ref, x_ref[0].astype(F32).reshape(width * rows, chans))
    wait_weights(2)
    for first in firsts:
        total = sum_ref[first * WP : (first + BLOCK) * WP] + product(xa_ref, first, v_ref, 0)
        finish_rows(total, first, flat_ref, bias_ref[...], width, rows, y_ref, rim_ref)
    wait_all(loads[3])


def edge_part(side, src_ref, v_ref, coef_ref, rim0_ref, rim1_ref, pad_ref, halo_ref):
    _, width, chans = rim0_ref.shape
    row, col = tile_place()
    last = lax.div(lax.axis_size("tile"), TCOL) - 1
    inside = (row > 0) if side == 0 else (row < last)
    clear_tail(pad_ref, width)
    for k in range(4):
        cells = src_ref[k].astype(F32)
        if k >= 2:
            f = k - 2
            cells = activated(cells, coef_ref[2 * f : 2 * f + 1], coef_ref[2 * f + 1 : 2 * f + 2])
        at = lax.broadcasted_iota(jnp.int32, cells.shape, 0)
        keep = (at < width) | ((at == width) & (col > 0)) | ((at == width + 1) & (col < TCOL - 1))
        cells = jnp.where(keep & inside, cells, 0.0)
        pad_ref[k, 8 : 8 + width, :] = cells[0:width]
        pad_ref[k, 7:8, :] = cells[width : width + 1]
        pad_ref[k, 8 + width : 9 + width, :] = cells[width + 1 : width + 2]
        for b in range(3):
            halo_ref[k, :, b * chans : (b + 1) * chans] = pad_ref[k, 7 + b : 7 + b + WP, :].astype(BF16)
    parts = [jnp.dot(halo_ref[k], v_ref[2 * side, :, lo * chans : hi * chans], preferred_element_type=F32)
             for k, (lo, hi) in enumerate(((2, 3), (1, 3), (0, 2), (0, 1)))]
    total0 = parts[0] + parts[1][:, :chans] + parts[2][:, :chans]
    total1 = parts[1][:, chans:] + parts[2][:, chans:] + parts[3]
    return ((rim0_ref[side] + total0[:width]).astype(BF16), (rim1_ref[side] + total1[:width]).astype(BF16))


def half_kernel(side, x_ref, left_ref, right_ref, beyond_ref, v_ref, x1_ref, xa0_ref, coef_ref, bias_ref, rim0_ref, *refs):
    if side == 0:
        y_ref, new_ref, xa_ref, pad_ref, flat_ref, rim1_ref, halo_ref = refs
        frame_taps(1, x_ref, left_ref, right_ref, coef_ref[2:3], coef_ref[3:4], pad_ref, flat_ref, new_ref, xa_ref)
    else:
        xa_ref, y_ref, pad_ref, flat_ref, rim1_ref, halo_ref = refs
    _, width, rows, chans = x_ref.shape
    put_lines(flat_ref, x_ref[1].astype(F32).reshape(width * rows, chans))
    first = side * BLOCK
    total = (product(x1_ref, first, v_ref, 2) + product(xa0_ref, first, v_ref, 1)
             + product(xa_ref, first, v_ref, 0))
    finish_rows(total, first, flat_ref, bias_ref[...], width, rows, y_ref.at[pl.ds(0, BLOCK - 1)], rim1_ref, side * (BLOCK - 1))
    y_ref[BLOCK - 1], y_ref[BLOCK] = edge_part(
        side, beyond_ref, v_ref, coef_ref, rim0_ref, rim1_ref, pad_ref, halo_ref)


def spread_kernel(y0_ref, half_ref, new0_ref, new1_ref, flat_ref, new_ref):
    new_ref[0] = new0_ref[...]
    new_ref[1] = new1_ref[...]
    inner, width, _ = y0_ref.shape
    rows = inner + 2
    for r in range(inner):
        put_row(flat_ref.at[0], r + 1, rows, width, y0_ref[r].astype(F32))
    for f in range(2):
        put_row(flat_ref.at[f], 0, rows, width, half_ref[BLOCK - 1 + f].astype(F32))
    for at in range(BLOCK - 1):
        put_row(flat_ref.at[1], at + 1, rows, width, half_ref[at].astype(F32))


def join_kernel(flat_ref, half_ref, out_ref, scr_ref):
    _, width, rows, chans = out_ref.shape
    line = lax.broadcasted_iota(jnp.int32, (width * rows, LANES), 0) & (rows - 1)
    for f in range(2):
        put_row(scr_ref.at[f], rows - 1, rows, width, half_ref[BLOCK - 1 + f].astype(F32))
    for at in range(BLOCK - 1):
        put_row(scr_ref.at[1], rows - BLOCK + at, rows, width, half_ref[at].astype(F32))
    for f, late in ((0, line == rows - 1), (1, line >= rows - BLOCK)):
        for j in range(flat_ref.shape[1]):
            whole = jnp.where(late, scr_ref[f, j], flat_ref[f, j])
            out_ref[f, :, :, j * LANES : (j + 1) * LANES] = whole.astype(BF16).reshape(width, rows, LANES)


def in_hbm(x):
    return pltpu.with_memory_space_constraint(x, pltpu.HBM)


def on_device(frames_in, cache, kernel, gain, conv_bias):
    x = in_hbm(jnp.transpose(frames_in[0][:, 0], (0, 2, 1, 3)))
    c = in_hbm(jnp.transpose(cache[0][:, 0], (0, 2, 1, 3)))
    frames, width, rows, chans = x.shape
    tiles = lax.axis_size("tile")
    sections = lax.axis_size("section")
    weights = in_hbm(kernel.reshape(3, 3, 3 * chans, chans))
    inner = rows - 2
    sds = jax.ShapeDtypeStruct
    HBM = pl.BlockSpec(memory_space=pltpu.HBM)
    DMA = pltpu.SemaphoreType.DMA

    taps = pltpu.VMEM((rows + 2, WP, 3 * chans), BF16)
    acc = (rows * WP, chans)
    cols = sds((4, rows, chans), F32)
    frame = pltpu.VMEM((width, rows, chans), BF16)
    both = pltpu.VMEM((frames, width, rows, chans), BF16)
    pad = pltpu.VMEM((rows, 80, chans), F32)
    flat = pltpu.VMEM((chans // LANES, width * rows, LANES), F32)
    rim = pltpu.VMEM((2, width, chans), F32)
    edge_rows = sds((4, WP, chans), BF16)

    def call(body, name, us, in_specs, out_specs, out_shape, scratch, aliases={}):
        return pl.pallas_call(body, input_output_aliases=aliases, out_shape=out_shape, in_specs=in_specs, out_specs=out_specs,
                              scratch_shapes=scratch, compiler_params=params(), name=name, cost_estimate=cost(us))

    stat, first_col, last_col = call(
        first_kernel, "local_stats", 1, [HBM] * 2, [VMEM] * 3,
        (sds((tiles, 1, 128), F32), sds((4, rows, chans), BF16), sds((4, rows, chans), BF16)),
        [both, pltpu.VMEM((2, 2, rows, chans), BF16), DMA((2, PARTS)), DMA((2, 2))],
    )(x, c)
    stats = lax.all_to_all(stat, "tile", 0, 0, tiled=True)
    next_col = [(i, i - i % TCOL + (i + 1) % TCOL) for i in range(tiles)]
    next_row = [(i, (i + TCOL) % tiles) for i in range(tiles)]
    back = lambda pairs: [(j, i) for i, j in pairs]
    from_left = lax.ppermute(last_col, "tile", next_col)
    from_right = lax.ppermute(first_col, "tile", back(next_col))
    bottom, top, left, right = call(
        rows_kernel, "pack_rows", 2, [HBM, HBM, VMEM, VMEM], [VMEM] * 4, (edge_rows, edge_rows, cols, cols),
        [pltpu.VMEM((4, width, rows, chans), BF16), flat, DMA((4, PARTS))],
    )(c, x, from_left, from_right)
    above = lax.ppermute(bottom, "tile", next_row)
    below = lax.ppermute(top, "tile", back(next_row))
    onward = [(i, (i + 1) % sections) for i in range(sections)]
    y0, rim0, new0, v, coef, xv, x1, xa0 = call(
        functools.partial(frame0_kernel, tiles), "frame0", 10, [VMEM, HBM, HBM, VMEM, VMEM, HBM, VMEM, VMEM], [VMEM] * 8,
        (sds((inner, width, chans), BF16), rim, frame, pltpu.VMEM((3, 3 * chans, 3 * chans), BF16),
         pltpu.VMEM((8, chans), F32), both, taps, taps),
        [both, taps, pltpu.VMEM(acc, F32), pad, flat, DMA((4, PARTS)), DMA((3, 3))],
    )(stats, c, x, left, right, weights, gain, conv_bias)
    y0 = lax.ppermute(y0, "section", onward)
    half = sds((BLOCK + 1, width, chans), BF16)
    halo = pltpu.VMEM((4, WP, 3 * chans), BF16)
    half_a, new1, xa1 = call(
        functools.partial(half_kernel, 0), "frame1_first", 4, [VMEM] * 10, [VMEM] * 3, (half, frame, taps),
        [pad, flat, rim, halo],
    )(xv, left, right, above, v, x1, xa0, coef, conv_bias, rim0)
    half_a = lax.ppermute(half_a, "section", onward)
    half_b = call(
        functools.partial(half_kernel, 1), "frame1_second", 4, [VMEM] * 11, VMEM, half, [pad, flat, rim, halo],
    )(xv, left, right, below, v, x1, xa0, coef, conv_bias, rim0, xa1)
    half_b = lax.ppermute(half_b, "section", onward)
    spread, new = call(
        spread_kernel, "spread_rows", 10, [VMEM] * 4, [VMEM] * 2,
        (pltpu.VMEM((frames, chans // LANES, width * rows, LANES), F32), sds((frames, width, rows, chans), BF16)), [],
    )(y0, half_a, new0, new1)
    handed = call(
        join_kernel, "join_rows", 1, [VMEM] * 2, VMEM, sds((frames, width, rows, chans), BF16),
        [pltpu.VMEM((frames, chans // LANES, width * rows, LANES), F32)],
    )(spread, half_b)
    handed = jnp.transpose(handed, (0, 2, 1, 3))
    new = jnp.transpose(new, (0, 2, 1, 3))
    return (handed[None, :, None], new[None, :, None])


def solution(mesh):
    tiled = P("section", None, "tile", None, None, None)
    in_specs = (tiled, tiled, P("section", None, None, None, None, None), P("section", None), P("section", None))
    return jax.shard_map(
        on_device, mesh=mesh, in_specs=in_specs, out_specs=(tiled, tiled), check_vma=False
    )
```

```python
import functools

import jax
import jax.numpy as jnp
from jax import lax
from jax.experimental import pallas as pl
from jax.experimental.pallas import tpu as pltpu
from jax.sharding import PartitionSpec as P

GROUPS = 32
TCOL = 4
EPS = 1e-06
WP = 64
F32 = jnp.float32
BF16 = jnp.bfloat16
VMEM = pl.BlockSpec(memory_space=pltpu.VMEM)
ANY = pl.BlockSpec(memory_space=pl.ANY)
LIMIT = 20 * 1024 * 1024


def cost(us):
    return pl.CostEstimate(flops=int(us * 1e9), bytes_accessed=int(us * 3e6), transcendentals=0)


def params():
    return pltpu.CompilerParams(vmem_limit_bytes=LIMIT)


def split3(x):
    high = x.astype(BF16)
    rest = x - high.astype(F32)
    mid = rest.astype(BF16)
    low = (rest - mid.astype(F32)).astype(BF16)
    return high, mid, low


def exact_dot(x, onehot):
    pad = jnp.zeros_like(x)
    parts = split3(x)
    lhs = jnp.concatenate([jnp.concatenate([p.astype(F32), pad], axis=0) for p in parts], axis=0)
    got = jnp.dot(lhs.astype(BF16), onehot, preferred_element_type=F32)
    return got[0:8] + got[16:24] + got[32:40]


def to_group(chans):
    size = chans // GROUPS
    chan = lax.broadcasted_iota(jnp.int32, (chans, 128), 0)
    first = (lax.broadcasted_iota(jnp.int32, (chans, 128), 1) & (GROUPS - 1)) * size
    return jnp.where((chan >= first) & (chan < first + size), 1.0, 0.0).astype(BF16)


def same_group(chans):
    size = chans // GROUPS
    row = lax.broadcasted_iota(jnp.int32, (chans, 1), 0)
    col = lax.broadcasted_iota(jnp.int32, (1, chans), 1)
    of = lambda c: (c * ((1 << 18) // size + 1)) >> 18
    return jnp.where(of(row) == of(col), 1.0, 0.0).astype(BF16)


def from_group(chans, block):
    size = chans // GROUPS
    lane = lax.broadcasted_iota(jnp.int32, (128, chans), 0)
    chan = lax.broadcasted_iota(jnp.int32, (128, chans), 1)
    first = (lane & (GROUPS - 1)) * size
    hit = (chan >= first) & (chan < first + size) & ((lane >> 5) == block)
    return jnp.where(hit, 1.0, 0.0).astype(BF16)


PARTS = 4


def fetch(hbm_ref, f, vmem_ref, sems):
    step = hbm_ref.shape[1] // PARTS
    copies = [pltpu.make_async_copy(hbm_ref.at[f, pl.ds(p * step, step)], vmem_ref.at[pl.ds(p * step, step)],
                                    sems.at[p]) for p in range(PARTS)]
    for copy in copies:
        copy.start()
    return copies


def wait_all(copies):
    for copy in copies:
        copy.wait()


def first_kernel(x_hbm, c_hbm, stat_ref, first_ref, last_ref, x_ref, edge_ref, sems, edge_sems):
    frames, width, rows, chans = x_ref.shape
    loads = [fetch(x_hbm, f, x_ref.at[f], sems.at[f]) for f in range(frames)]
    edges = []
    for f in range(2):
        for at, w in ((0, 0), (1, width - 1)):
            edges.append(pltpu.make_async_copy(c_hbm.at[f, w], edge_ref.at[f, at], edge_sems.at[f, at]))
    for copy in edges:
        copy.start()
    size = chans // GROUPS
    count = rows * width
    every, same = to_group(chans), same_group(chans)
    sums, squares = [], []
    for f in range(frames):
        wait_all(loads[f])
        x = x_ref[f].astype(F32)
        total = jnp.sum(jnp.sum(x, axis=0), axis=0, keepdims=True)
        dev = x - (total * (1.0 / count))[None]
        sums.append(total)
        squares.append(jnp.sum(jnp.sum(dev * dev, axis=0), axis=0, keepdims=True))
    wait_all(edges)
    for k in range(4):
        first_ref[k] = edge_ref[k, 0] if k < 2 else x_ref[k - 2, 0]
        last_ref[k] = edge_ref[k, 1] if k < 2 else x_ref[k - 2, width - 1]
    zero = jnp.zeros((1, chans), F32)
    both = jnp.concatenate(sums + [zero] * 6, axis=0)
    spread = exact_dot(both, same)
    off = both * (1.0 / count) - spread * (1.0 / (count * size))
    square = jnp.concatenate(squares + [zero] * 6, axis=0) + count * off * off
    row = lax.broadcasted_iota(jnp.int32, (8, 128), 0)
    lane = lax.broadcasted_iota(jnp.int32, (8, 128), 1)
    mix_sum = exact_dot(both, every)
    mix_square = exact_dot(square, every)
    kind = lane >> 5
    mixed = jnp.where((row == 0) & (kind == 0), mix_sum, 0.0)
    mixed = mixed + jnp.where((row == 1) & (kind == 2), mix_sum, 0.0)
    mixed = mixed + jnp.where((row == 0) & (kind == 1), mix_square, 0.0)
    mixed = mixed + jnp.where((row == 1) & (kind == 3), mix_square, 0.0)
    line = jnp.sum(mixed, axis=0, keepdims=True)
    stat_ref[...] = jnp.broadcast_to(line[None], stat_ref.shape)


LANES = 128


def put_lines(flat_ref, lines):
    for j in range(flat_ref.shape[0]):
        flat_ref[j] = lines[:, j * LANES : (j + 1) * LANES]


def get_row(flat_ref, r, rows, width):
    return jnp.concatenate(
        [flat_ref[j, pl.ds(r, width, stride=rows), :] for j in range(flat_ref.shape[0])], axis=1)


def put_row(flat_ref, r, rows, width, value):
    for j in range(flat_ref.shape[0]):
        flat_ref[j, pl.ds(r, width, stride=rows), :] = value[:, j * LANES : (j + 1) * LANES]


def build_taps(flat_ref, left, right, pad_ref, out_ref, rows, width):
    chans = pad_ref.shape[-1]
    for r in range(rows):
        pad_ref[r, 8 : 8 + width, :] = get_row(flat_ref, r, rows, width)
        pad_ref[r, 7:8, :] = left[r : r + 1]
        pad_ref[r, 8 + width : 9 + width, :] = right[r : r + 1]
    for b in range(3):
        out_ref[1 : 1 + rows, :, b * chans : (b + 1) * chans] = pad_ref[:, 7 + b : 7 + b + WP, :].astype(BF16)
    out_ref[0] = jnp.zeros_like(out_ref[0])
    out_ref[rows + 1] = jnp.zeros_like(out_ref[0])


def clear_tail(pad_ref, width):
    pad_ref[:, 8 + width :, :] = jnp.zeros_like(pad_ref[:, 8 + width :, :])


def tile_place():
    tile = lax.axis_index("tile")
    return lax.div(tile, TCOL), lax.rem(tile, TCOL)


BLOCK = 4


def wide_taps(taps_ref, first):
    return jnp.concatenate([taps_ref[first + a : first + a + BLOCK].reshape(BLOCK * WP, -1) for a in range(3)], axis=1)


def product(taps_ref, first, v_ref, at):
    return jnp.dot(wide_taps(taps_ref, first), tap_weights(v_ref, at, at + 1), preferred_element_type=F32)


def tap_weights(v_ref, lo, hi):
    chans = v_ref.shape[1] // 3
    return v_ref[:, :, lo * chans : hi * chans].reshape(9 * chans, (hi - lo) * chans)


def rows_kernel(c_hbm, x_hbm, from_left_ref, from_right_ref, bottom_ref, top_ref, left_ref, right_ref,
                frame_ref, flat_ref, sems):
    _, width, rows, chans = frame_ref.shape
    loads = [fetch(c_hbm if k < 2 else x_hbm, k % 2, frame_ref.at[k], sems.at[k]) for k in range(4)]
    _, col = tile_place()
    left_ref[...] = jnp.where(col > 0, from_left_ref[...].astype(F32), 0.0)
    right_ref[...] = jnp.where(col < TCOL - 1, from_right_ref[...].astype(F32), 0.0)
    for k in range(4):
        wait_all(loads[k])
        put_lines(flat_ref, frame_ref[k].astype(F32).reshape(width * rows, chans))
        for out_ref, r in ((bottom_ref, rows - 1), (top_ref, 0)):
            last = jnp.concatenate([left_ref[k, r : r + 1], right_ref[k, r : r + 1],
                                    jnp.zeros((WP - width - 2, chans), F32)], axis=0)
            line = jnp.concatenate([get_row(flat_ref, r, rows, width), last], axis=0)
            out_ref[k] = line.astype(BF16)


def silu(v):
    return v / (1.0 + jnp.exp(-v))


def activated(x, scale, shift):
    return silu(x * scale + shift)


def frame_taps(f, x_ref, left_ref, right_ref, scale, shift, pad_ref, flat_ref, new_ref, out_ref):
    _, width, rows, chans = x_ref.shape
    _, col = tile_place()
    act = activated(x_ref[f].astype(F32).reshape(width * rows, chans), scale, shift)
    put_lines(flat_ref, act)
    new_ref[...] = act.astype(BF16).reshape(width, rows, chans)
    left = activated(left_ref[2 + f], scale, shift)
    right = activated(right_ref[2 + f], scale, shift)
    left = jnp.where(col > 0, left, 0.0)
    right = jnp.where(col < TCOL - 1, right, 0.0)
    clear_tail(pad_ref, width)
    build_taps(flat_ref, left, right, pad_ref, out_ref, rows, width)


def put_cells(line_ref, at, value):
    line_ref[at * value.shape[0] : (at + 1) * value.shape[0], :] = value


def finish_rows(total, first, flat_ref, bias, width, rows, line_ref, rim_ref, skip=0):
    for at in range(BLOCK):
        r = first + at
        whole = get_row(flat_ref, r, rows, width) + bias + total[at * WP : at * WP + width]
        if r in (0, rows - 1):
            rim_ref[r // (rows - 1)] = whole
        else:
            put_cells(line_ref, r - 1 - skip, whole)


def frame0_kernel(tiles, stat_ref, c_hbm, x_hbm, left_ref, right_ref, w_hbm, gain_ref, bias_ref,
                  y_ref, rim_ref, new_ref, v_ref, coef_ref, x_ref, x1_ref, xa_ref,
                  c_ref, x0_ref, sum_ref, pad_ref, flat_ref, line_ref, frame_sems, sems):
    _, width, rows, chans = x_ref.shape
    loads = [fetch(c_hbm, 0, c_ref.at[0], frame_sems.at[0]), fetch(c_hbm, 1, c_ref.at[1], frame_sems.at[1]),
             fetch(x_hbm, 0, x_ref.at[0], frame_sems.at[2])]
    copies = {}
    for t in range(3):
        for a in range(3):
            copies[t, a] = pltpu.make_async_copy(
                w_hbm.at[t, a], v_ref.at[a, :, (2 - t) * chans : (3 - t) * chans], sems.at[t, a])
            copies[t, a].start()

    def wait_weights(t):
        for a in range(3):
            copies[t, a].wait()

    loads.append(fetch(x_hbm, 1, x_ref.at[1], frame_sems.at[3]))
    part = rows * width * (chans // GROUPS)
    count = part * tiles
    stat = stat_ref[...].reshape(tiles, 128)
    moved = pltpu.roll(stat, GROUPS, 1)
    mean = jnp.sum(stat, axis=0, keepdims=True) * (1.0 / count)
    mean_moved = jnp.sum(moved, axis=0, keepdims=True) * (1.0 / count)
    off = moved * (1.0 / part) - mean_moved
    var = jnp.sum(stat + part * off * off, axis=0, keepdims=True) * (1.0 / count)
    lane = lax.broadcasted_iota(jnp.int32, (1, 128), 1)
    is_mean = ((lane >> 5) & 1) == 0
    both = jnp.where(is_mean, mean, lax.rsqrt(jnp.maximum(var, 0.0) + EPS))
    both = jnp.broadcast_to(both, (8, 128))
    gain = gain_ref[...]
    for f in range(2):
        means = exact_dot(both, from_group(chans, 2 * f))[0:1]
        rstds = exact_dot(both, from_group(chans, 2 * f + 1))[0:1]
        scale = rstds * gain
        coef_ref[2 * f : 2 * f + 1, :] = scale
        coef_ref[2 * f + 1 : 2 * f + 2, :] = -means * scale
    clear_tail(pad_ref, width)
    for k, out_ref in ((0, x0_ref), (1, x1_ref)):
        wait_all(loads[k])
        put_lines(flat_ref, c_ref[k].astype(F32).reshape(width * rows, chans))
        build_taps(flat_ref, left_ref[k], right_ref[k], pad_ref, out_ref, rows, width)
    wait_all(loads[2])
    frame_taps(0, x_ref, left_ref, right_ref, coef_ref[0:1], coef_ref[1:2], pad_ref, flat_ref, new_ref, xa_ref)
    put_lines(flat_ref, x_ref[0].astype(F32).reshape(width * rows, chans))
    firsts = range(0, rows, BLOCK)
    wait_weights(0)
    for first in firsts:
        sum_ref[first * WP : (first + BLOCK) * WP] = product(x0_ref, first, v_ref, 2)
    wait_weights(1)
    for first in firsts:
        sum_ref[first * WP : (first + BLOCK) * WP] += product(x1_ref, first, v_ref, 1)
    wait_weights(2)
    for first in firsts:
        total = sum_ref[first * WP : (first + BLOCK) * WP] + product(xa_ref, first, v_ref, 0)
        finish_rows(total, first, flat_ref, bias_ref[...], width, rows, line_ref, rim_ref)
    y_ref[...] = line_ref[...].astype(BF16)
    wait_all(loads[3])


def edge_part(side, src_ref, v_ref, coef_ref, rim0_ref, rim1_ref, pad_ref, halo_ref):
    _, width, chans = rim0_ref.shape
    row, col = tile_place()
    last = lax.div(lax.axis_size("tile"), TCOL) - 1
    inside = (row > 0) if side == 0 else (row < last)
    clear_tail(pad_ref, width)
    for k in range(4):
        cells = src_ref[k].astype(F32)
        if k >= 2:
            f = k - 2
            cells = activated(cells, coef_ref[2 * f : 2 * f + 1], coef_ref[2 * f + 1 : 2 * f + 2])
        at = lax.broadcasted_iota(jnp.int32, cells.shape, 0)
        keep = (at < width) | ((at == width) & (col > 0)) | ((at == width + 1) & (col < TCOL - 1))
        cells = jnp.where(keep & inside, cells, 0.0)
        pad_ref[k, 8 : 8 + width, :] = cells[0:width]
        pad_ref[k, 7:8, :] = cells[width : width + 1]
        pad_ref[k, 8 + width : 9 + width, :] = cells[width + 1 : width + 2]
        for b in range(3):
            halo_ref[k, :, b * chans : (b + 1) * chans] = pad_ref[k, 7 + b : 7 + b + WP, :].astype(BF16)
    parts = [jnp.dot(halo_ref[k], v_ref[2 * side, :, lo * chans : hi * chans], preferred_element_type=F32)
             for k, (lo, hi) in enumerate(((2, 3), (1, 3), (0, 2), (0, 1)))]
    total0 = parts[0] + parts[1][:, :chans] + parts[2][:, :chans]
    total1 = parts[1][:, chans:] + parts[2][:, chans:] + parts[3]
    return rim0_ref[side] + total0[:width], rim1_ref[side] + total1[:width]


def half_kernel(side, x_ref, left_ref, right_ref, beyond_ref, v_ref, x1_ref, xa0_ref, coef_ref, bias_ref, rim0_ref, *refs):
    if side == 0:
        y_ref, new_ref, xa_ref, pad_ref, flat_ref, rim1_ref, halo_ref, line_ref = refs
        frame_taps(1, x_ref, left_ref, right_ref, coef_ref[2:3], coef_ref[3:4], pad_ref, flat_ref, new_ref, xa_ref)
    else:
        xa_ref, y_ref, pad_ref, flat_ref, rim1_ref, halo_ref, line_ref = refs
    _, width, rows, chans = x_ref.shape
    put_lines(flat_ref, x_ref[1].astype(F32).reshape(width * rows, chans))
    first = side * BLOCK
    total = (product(x1_ref, first, v_ref, 2) + product(xa0_ref, first, v_ref, 1)
             + product(xa_ref, first, v_ref, 0))
    finish_rows(total, first, flat_ref, bias_ref[...], width, rows, line_ref, rim1_ref, side * (BLOCK - 1))
    for f, row in enumerate(edge_part(side, beyond_ref, v_ref, coef_ref, rim0_ref, rim1_ref, pad_ref, halo_ref)):
        put_cells(line_ref, BLOCK - 1 + f, row)
    y_ref[...] = line_ref[...].astype(BF16)


def spread_kernel(y0_ref, half_ref, new0_ref, new1_ref, flat_ref, new_ref):
    new_ref[0] = new0_ref[...]
    new_ref[1] = new1_ref[...]
    _, width, rows, _ = new_ref.shape
    y0, half = y0_ref[...].astype(F32), half_ref[...].astype(F32)
    for r in range(rows - 2):
        put_row(flat_ref.at[0], r + 1, rows, width, y0[r * width : (r + 1) * width])
    for f in range(2):
        put_row(flat_ref.at[f], 0, rows, width, half[(BLOCK - 1 + f) * width : (BLOCK + f) * width])
    for at in range(BLOCK - 1):
        put_row(flat_ref.at[1], at + 1, rows, width, half[at * width : (at + 1) * width])


def join_kernel(flat_ref, half_ref, out_hbm, scr_ref, out_ref, sems):
    _, width, rows, chans = out_ref.shape
    line = lax.broadcasted_iota(jnp.int32, (width * rows, LANES), 0) & (rows - 1)
    half = half_ref[...].astype(F32)
    copies = []
    for f, late in ((0, line == rows - 1), (1, line >= rows - BLOCK)):
        put_row(scr_ref.at[f], rows - 1, rows, width, half[(BLOCK - 1 + f) * width : (BLOCK + f) * width])
        if f == 1:
            for at in range(BLOCK - 1):
                put_row(scr_ref.at[1], rows - BLOCK + at, rows, width, half[at * width : (at + 1) * width])
        for j in range(flat_ref.shape[1]):
            whole = jnp.where(late, scr_ref[f, j], flat_ref[f, j])
            out_ref[f, :, :, j * LANES : (j + 1) * LANES] = whole.astype(BF16).reshape(width, rows, LANES)
        copies.append(pltpu.make_async_copy(out_ref.at[f], out_hbm.at[f], sems.at[f]))
        copies[-1].start()
    wait_all(copies)


def in_hbm(x):
    return pltpu.with_memory_space_constraint(x, pltpu.HBM)


def on_device(frames_in, cache, kernel, gain, conv_bias):
    x = in_hbm(jnp.transpose(frames_in[0][:, 0], (0, 2, 1, 3)))
    c = in_hbm(jnp.transpose(cache[0][:, 0], (0, 2, 1, 3)))
    frames, width, rows, chans = x.shape
    tiles = lax.axis_size("tile")
    sections = lax.axis_size("section")
    weights = in_hbm(kernel.reshape(3, 3, 3 * chans, chans))
    inner = rows - 2
    sds = jax.ShapeDtypeStruct
    HBM = pl.BlockSpec(memory_space=pltpu.HBM)
    DMA = pltpu.SemaphoreType.DMA

    taps = pltpu.VMEM((rows + 2, WP, 3 * chans), BF16)
    acc = (rows * WP, chans)
    cols = sds((4, rows, chans), F32)
    frame = pltpu.VMEM((width, rows, chans), BF16)
    both = pltpu.VMEM((frames, width, rows, chans), BF16)
    pad = pltpu.VMEM((rows, 80, chans), F32)
    flat = pltpu.VMEM((chans // LANES, width * rows, LANES), F32)
    rim = pltpu.VMEM((2, width, chans), F32)
    edge_rows = sds((4, WP, chans), BF16)

    def call(body, name, us, in_specs, out_specs, out_shape, scratch, aliases={}):
        return pl.pallas_call(body, input_output_aliases=aliases, out_shape=out_shape, in_specs=in_specs, out_specs=out_specs,
                              scratch_shapes=scratch, compiler_params=params(), name=name, cost_estimate=cost(us))

    stat, first_col, last_col = call(
        first_kernel, "local_stats", 1, [HBM] * 2, [VMEM] * 3,
        (sds((tiles, 1, 128), F32), sds((4, rows, chans), BF16), sds((4, rows, chans), BF16)),
        [both, pltpu.VMEM((2, 2, rows, chans), BF16), DMA((2, PARTS)), DMA((2, 2))],
    )(x, c)
    stats = lax.all_to_all(stat, "tile", 0, 0, tiled=True)
    next_col = [(i, i - i % TCOL + (i + 1) % TCOL) for i in range(tiles)]
    next_row = [(i, (i + TCOL) % tiles) for i in range(tiles)]
    back = lambda pairs: [(j, i) for i, j in pairs]
    from_left = lax.ppermute(last_col, "tile", next_col)
    from_right = lax.ppermute(first_col, "tile", back(next_col))
    bottom, top, left, right = call(
        rows_kernel, "pack_rows", 2, [HBM, HBM, VMEM, VMEM], [VMEM] * 4, (edge_rows, edge_rows, cols, cols),
        [pltpu.VMEM((4, width, rows, chans), BF16), flat, DMA((4, PARTS))],
    )(c, x, from_left, from_right)
    above = lax.ppermute(bottom, "tile", next_row)
    below = lax.ppermute(top, "tile", back(next_row))
    onward = [(i, (i + 1) % sections) for i in range(sections)]
    y0, rim0, new0, v, coef, xv, x1, xa0 = call(
        functools.partial(frame0_kernel, tiles), "frame0", 10, [VMEM, HBM, HBM, VMEM, VMEM, HBM, VMEM, VMEM], [VMEM] * 8,
        (sds((inner * width, chans), BF16), rim, frame, pltpu.VMEM((3, 3 * chans, 3 * chans), BF16),
         pltpu.VMEM((8, chans), F32), both, taps, taps),
        [both, taps, pltpu.VMEM(acc, F32), pad, flat, pltpu.VMEM((inner * width, chans), F32),
         DMA((4, PARTS)), DMA((3, 3))],
    )(stats, c, x, left, right, weights, gain, conv_bias)
    y0 = lax.ppermute(y0, "section", onward)
    half = sds(((BLOCK + 1) * width, chans), BF16)
    lines = pltpu.VMEM(((BLOCK + 1) * width, chans), F32)
    halo = pltpu.VMEM((4, WP, 3 * chans), BF16)
    half_a, new1, xa1 = call(
        functools.partial(half_kernel, 0), "frame1_first", 4, [VMEM] * 10, [VMEM] * 3, (half, frame, taps),
        [pad, flat, rim, halo, lines],
    )(xv, left, right, above, v, x1, xa0, coef, conv_bias, rim0)
    half_a = lax.ppermute(half_a, "section", onward)
    half_b = call(
        functools.partial(half_kernel, 1), "frame1_second", 4, [VMEM] * 11, VMEM, half, [pad, flat, rim, halo, lines],
    )(xv, left, right, below, v, x1, xa0, coef, conv_bias, rim0, xa1)
    half_b = lax.ppermute(half_b, "section", onward)
    spread, new = call(
        spread_kernel, "spread_rows", 10, [VMEM] * 4, [VMEM] * 2,
        (pltpu.VMEM((frames, chans // LANES, width * rows, LANES), F32), sds((frames, width, rows, chans), BF16)), [],
    )(y0, half_a, new0, new1)
    handed = call(
        join_kernel, "join_rows", 1, [VMEM] * 2, HBM, sds((frames, width, rows, chans), BF16),
        [pltpu.VMEM((frames, chans // LANES, width * rows, LANES), F32), both, DMA((2,))],
    )(spread, half_b)
    handed = jnp.transpose(handed, (0, 2, 1, 3))
    new = jnp.transpose(new, (0, 2, 1, 3))
    return (handed[None, :, None], new[None, :, None])


def solution(mesh):
    tiled = P("section", None, "tile", None, None, None)
    in_specs = (tiled, tiled, P("section", None, None, None, None, None), P("section", None), P("section", None))
    return jax.shard_map(
        on_device, mesh=mesh, in_specs=in_specs, out_specs=(tiled, tiled), check_vma=False
    )
```

```python
import functools

import jax
import jax.numpy as jnp
from jax import lax
from jax.experimental import pallas as pl
from jax.experimental.pallas import tpu as pltpu
from jax.sharding import PartitionSpec as P

GROUPS = 32
TCOL = 4
EPS = 1e-06
WP = 64
F32 = jnp.float32
BF16 = jnp.bfloat16
VMEM = pl.BlockSpec(memory_space=pltpu.VMEM)
ANY = pl.BlockSpec(memory_space=pl.ANY)
LIMIT = 20 * 1024 * 1024


def cost(us):
    return pl.CostEstimate(flops=int(us * 1e9), bytes_accessed=int(us * 3e6), transcendentals=0)


def params():
    return pltpu.CompilerParams(vmem_limit_bytes=LIMIT)


def split3(x):
    high = x.astype(BF16)
    rest = x - high.astype(F32)
    mid = rest.astype(BF16)
    low = (rest - mid.astype(F32)).astype(BF16)
    return high, mid, low


def exact_dot(x, onehot):
    pad = jnp.zeros_like(x)
    parts = split3(x)
    lhs = jnp.concatenate([jnp.concatenate([p.astype(F32), pad], axis=0) for p in parts], axis=0)
    got = jnp.dot(lhs.astype(BF16), onehot, preferred_element_type=F32)
    return got[0:8] + got[16:24] + got[32:40]


def to_group(chans):
    size = chans // GROUPS
    chan = lax.broadcasted_iota(jnp.int32, (chans, 128), 0)
    first = (lax.broadcasted_iota(jnp.int32, (chans, 128), 1) & (GROUPS - 1)) * size
    return jnp.where((chan >= first) & (chan < first + size), 1.0, 0.0).astype(BF16)


def same_group(chans):
    size = chans // GROUPS
    row = lax.broadcasted_iota(jnp.int32, (chans, 1), 0)
    col = lax.broadcasted_iota(jnp.int32, (1, chans), 1)
    of = lambda c: (c * ((1 << 18) // size + 1)) >> 18
    return jnp.where(of(row) == of(col), 1.0, 0.0).astype(BF16)


def from_group(chans, block):
    size = chans // GROUPS
    lane = lax.broadcasted_iota(jnp.int32, (128, chans), 0)
    chan = lax.broadcasted_iota(jnp.int32, (128, chans), 1)
    first = (lane & (GROUPS - 1)) * size
    hit = (chan >= first) & (chan < first + size) & ((lane >> 5) == block)
    return jnp.where(hit, 1.0, 0.0).astype(BF16)


PARTS = 4


def fetch(hbm_ref, f, vmem_ref, sems):
    step = hbm_ref.shape[1] // PARTS
    copies = [pltpu.make_async_copy(hbm_ref.at[f, pl.ds(p * step, step)], vmem_ref.at[pl.ds(p * step, step)],
                                    sems.at[p]) for p in range(PARTS)]
    for copy in copies:
        copy.start()
    return copies


def wait_all(copies):
    for copy in copies:
        copy.wait()


def first_kernel(x_hbm, c_hbm, stat_ref, first_ref, last_ref, x_ref, edge_ref, sems, edge_sems):
    frames, width, rows, chans = x_ref.shape
    loads = [fetch(x_hbm, f, x_ref.at[f], sems.at[f]) for f in range(frames)]
    edges = []
    for f in range(2):
        for at, w in ((0, 0), (1, width - 1)):
            edges.append(pltpu.make_async_copy(c_hbm.at[f, w], edge_ref.at[f, at], edge_sems.at[f, at]))
    for copy in edges:
        copy.start()
    size = chans // GROUPS
    count = rows * width
    every, same = to_group(chans), same_group(chans)
    sums, squares = [], []
    for f in range(frames):
        wait_all(loads[f])
        x = x_ref[f].astype(F32)
        total = jnp.sum(jnp.sum(x, axis=0), axis=0, keepdims=True)
        dev = x - (total * (1.0 / count))[None]
        sums.append(total)
        squares.append(jnp.sum(jnp.sum(dev * dev, axis=0), axis=0, keepdims=True))
    wait_all(edges)
    for k in range(4):
        first_ref[k] = edge_ref[k, 0] if k < 2 else x_ref[k - 2, 0]
        last_ref[k] = edge_ref[k, 1] if k < 2 else x_ref[k - 2, width - 1]
    zero = jnp.zeros((1, chans), F32)
    both = jnp.concatenate(sums + [zero] * 6, axis=0)
    spread = exact_dot(both, same)
    off = both * (1.0 / count) - spread * (1.0 / (count * size))
    square = jnp.concatenate(squares + [zero] * 6, axis=0) + count * off * off
    row = lax.broadcasted_iota(jnp.int32, (8, 128), 0)
    lane = lax.broadcasted_iota(jnp.int32, (8, 128), 1)
    mix_sum = exact_dot(both, every)
    mix_square = exact_dot(square, every)
    kind = lane >> 5
    mixed = jnp.where((row == 0) & (kind == 0), mix_sum, 0.0)
    mixed = mixed + jnp.where((row == 1) & (kind == 2), mix_sum, 0.0)
    mixed = mixed + jnp.where((row == 0) & (kind == 1), mix_square, 0.0)
    mixed = mixed + jnp.where((row == 1) & (kind == 3), mix_square, 0.0)
    line = jnp.sum(mixed, axis=0, keepdims=True)
    stat_ref[...] = jnp.broadcast_to(line[None], stat_ref.shape)


LANES = 128


def put_lines(flat_ref, lines):
    for j in range(flat_ref.shape[0]):
        flat_ref[j] = lines[:, j * LANES : (j + 1) * LANES]


def get_row(flat_ref, r, rows, width):
    return jnp.concatenate(
        [flat_ref[j, pl.ds(r, width, stride=rows), :] for j in range(flat_ref.shape[0])], axis=1)


def put_row(flat_ref, r, rows, width, value):
    for j in range(flat_ref.shape[0]):
        flat_ref[j, pl.ds(r, width, stride=rows), :] = value[:, j * LANES : (j + 1) * LANES]


def build_taps(flat_ref, left, right, pad_ref, out_ref, rows, width):
    chans = pad_ref.shape[-1]
    for r in range(rows):
        pad_ref[r, 8 : 8 + width, :] = get_row(flat_ref, r, rows, width)
        pad_ref[r, 7:8, :] = left[r : r + 1]
        pad_ref[r, 8 + width : 9 + width, :] = right[r : r + 1]
    for b in range(3):
        out_ref[1 : 1 + rows, :, b * chans : (b + 1) * chans] = pad_ref[:, 7 + b : 7 + b + WP, :].astype(BF16)
    out_ref[0] = jnp.zeros_like(out_ref[0])
    out_ref[rows + 1] = jnp.zeros_like(out_ref[0])


def clear_tail(pad_ref, width):
    pad_ref[:, 8 + width :, :] = jnp.zeros_like(pad_ref[:, 8 + width :, :])


def tile_place():
    tile = lax.axis_index("tile")
    return lax.div(tile, TCOL), lax.rem(tile, TCOL)


EARLY = 5


def wide_taps(taps_ref, first, count):
    return jnp.concatenate([taps_ref[first + a : first + a + count].reshape(count * WP, -1) for a in range(3)], axis=1)


def product(taps_ref, first, count, v_ref, at):
    return jnp.dot(wide_taps(taps_ref, first, count), tap_weights(v_ref, at, at + 1), preferred_element_type=F32)


def product_with(rim_taps_ref, rim, taps_ref, first, count, v_ref, at):
    lhs = jnp.concatenate([wide_taps(taps_ref, first, count), wide_taps(rim_taps_ref, rim, 1)], axis=0)
    return jnp.dot(lhs, tap_weights(v_ref, at, at + 1), preferred_element_type=F32)


def tap_weights(v_ref, lo, hi):
    chans = v_ref.shape[1] // 3
    return v_ref[:, :, lo * chans : hi * chans].reshape(9 * chans, (hi - lo) * chans)


def rows_kernel(c_hbm, x_hbm, from_left_ref, from_right_ref, bottom_ref, top_ref, left_ref, right_ref,
                frame_ref, flat_ref, sems):
    _, width, rows, chans = frame_ref.shape
    loads = [fetch(c_hbm if k < 2 else x_hbm, k % 2, frame_ref.at[k], sems.at[k]) for k in range(4)]
    _, col = tile_place()
    left_ref[...] = jnp.where(col > 0, from_left_ref[...].astype(F32), 0.0)
    right_ref[...] = jnp.where(col < TCOL - 1, from_right_ref[...].astype(F32), 0.0)
    for k in range(4):
        wait_all(loads[k])
        put_lines(flat_ref, frame_ref[k].astype(F32).reshape(width * rows, chans))
        for out_ref, r in ((bottom_ref, rows - 1), (top_ref, 0)):
            last = jnp.concatenate([left_ref[k, r : r + 1], right_ref[k, r : r + 1],
                                    jnp.zeros((WP - width - 2, chans), F32)], axis=0)
            line = jnp.concatenate([get_row(flat_ref, r, rows, width), last], axis=0)
            out_ref[k] = line.astype(BF16)


def silu(v):
    return v / (1.0 + jnp.exp(-v))


def activated(x, scale, shift):
    return silu(x * scale + shift)


def frame_taps(f, x_ref, left_ref, right_ref, scale, shift, pad_ref, flat_ref, new_ref, out_ref):
    _, width, rows, chans = x_ref.shape
    _, col = tile_place()
    act = activated(x_ref[f].astype(F32).reshape(width * rows, chans), scale, shift)
    put_lines(flat_ref, act)
    new_ref[...] = act.astype(BF16).reshape(width, rows, chans)
    left = activated(left_ref[2 + f], scale, shift)
    right = activated(right_ref[2 + f], scale, shift)
    left = jnp.where(col > 0, left, 0.0)
    right = jnp.where(col < TCOL - 1, right, 0.0)
    clear_tail(pad_ref, width)
    build_taps(flat_ref, left, right, pad_ref, out_ref, rows, width)


def put_cells(line_ref, at, value):
    line_ref[at * value.shape[0] : (at + 1) * value.shape[0], :] = value


def finish_rows(total, first, count, flat_ref, bias, width, rows, line_ref, at_line):
    rim = None
    for at in range(count):
        r = first + at
        whole = get_row(flat_ref, r, rows, width) + bias + total[at * WP : at * WP + width]
        if r in (0, rows - 1):
            rim = whole
        else:
            put_cells(line_ref, at_line, whole)
            at_line += 1
    return rim


def frame0_kernel(tiles, stat_ref, c_hbm, x_hbm, left_ref, right_ref, w_hbm, gain_ref, bias_ref,
                  y_ref, new_ref, v_ref, coef_ref, x_ref, x0_ref, x1_ref, xa_ref,
                  c_ref, sum_ref, pad_ref, flat_ref, line_ref, frame_sems, sems):
    _, width, rows, chans = x_ref.shape
    loads = [fetch(c_hbm, 0, c_ref.at[0], frame_sems.at[0]), fetch(c_hbm, 1, c_ref.at[1], frame_sems.at[1]),
             fetch(x_hbm, 0, x_ref.at[0], frame_sems.at[2])]
    copies = {}
    for t in range(3):
        for a in range(3):
            copies[t, a] = pltpu.make_async_copy(
                w_hbm.at[t, a], v_ref.at[a, :, (2 - t) * chans : (3 - t) * chans], sems.at[t, a])
            copies[t, a].start()

    def wait_weights(t):
        for a in range(3):
            copies[t, a].wait()

    loads.append(fetch(x_hbm, 1, x_ref.at[1], frame_sems.at[3]))
    part = rows * width * (chans // GROUPS)
    count = part * tiles
    stat = stat_ref[...].reshape(tiles, 128)
    moved = pltpu.roll(stat, GROUPS, 1)
    mean = jnp.sum(stat, axis=0, keepdims=True) * (1.0 / count)
    mean_moved = jnp.sum(moved, axis=0, keepdims=True) * (1.0 / count)
    off = moved * (1.0 / part) - mean_moved
    var = jnp.sum(stat + part * off * off, axis=0, keepdims=True) * (1.0 / count)
    lane = lax.broadcasted_iota(jnp.int32, (1, 128), 1)
    is_mean = ((lane >> 5) & 1) == 0
    both = jnp.where(is_mean, mean, lax.rsqrt(jnp.maximum(var, 0.0) + EPS))
    both = jnp.broadcast_to(both, (8, 128))
    gain = gain_ref[...]
    for f in range(2):
        means = exact_dot(both, from_group(chans, 2 * f))[0:1]
        rstds = exact_dot(both, from_group(chans, 2 * f + 1))[0:1]
        scale = rstds * gain
        coef_ref[2 * f : 2 * f + 1, :] = scale
        coef_ref[2 * f + 1 : 2 * f + 2, :] = -means * scale
    clear_tail(pad_ref, width)
    for k, out_ref in ((0, x0_ref), (1, x1_ref)):
        wait_all(loads[k])
        put_lines(flat_ref, c_ref[k].astype(F32).reshape(width * rows, chans))
        build_taps(flat_ref, left_ref[k], right_ref[k], pad_ref, out_ref, rows, width)
    wait_all(loads[2])
    frame_taps(0, x_ref, left_ref, right_ref, coef_ref[0:1], coef_ref[1:2], pad_ref, flat_ref, new_ref, xa_ref)
    put_lines(flat_ref, x_ref[0].astype(F32).reshape(width * rows, chans))
    step = (rows - 2) // 2
    firsts = (1, 1 + step)
    wait_weights(0)
    for first in firsts:
        sum_ref[first * WP : (first + step) * WP] = product(x0_ref, first, step, v_ref, 2)
    wait_weights(1)
    for first in firsts:
        sum_ref[first * WP : (first + step) * WP] += product(x1_ref, first, step, v_ref, 1)
    wait_weights(2)
    for first in firsts:
        total = sum_ref[first * WP : (first + step) * WP] + product(xa_ref, first, step, v_ref, 0)
        finish_rows(total, first, step, flat_ref, bias_ref[...], width, rows, line_ref, first - 1)
    y_ref[...] = line_ref[...].astype(BF16)
    wait_all(loads[3])


def edge_part(side, src_ref, v_ref, coef_ref, rim0, rim1, pad_ref, halo_ref):
    width, chans = rim0.shape
    row, col = tile_place()
    last = lax.div(lax.axis_size("tile"), TCOL) - 1
    inside = (row > 0) if side == 0 else (row < last)
    clear_tail(pad_ref, width)
    for k in range(4):
        cells = src_ref[k].astype(F32)
        if k >= 2:
            f = k - 2
            cells = activated(cells, coef_ref[2 * f : 2 * f + 1], coef_ref[2 * f + 1 : 2 * f + 2])
        at = lax.broadcasted_iota(jnp.int32, cells.shape, 0)
        keep = (at < width) | ((at == width) & (col > 0)) | ((at == width + 1) & (col < TCOL - 1))
        cells = jnp.where(keep & inside, cells, 0.0)
        pad_ref[k, 8 : 8 + width, :] = cells[0:width]
        pad_ref[k, 7:8, :] = cells[width : width + 1]
        pad_ref[k, 8 + width : 9 + width, :] = cells[width + 1 : width + 2]
        for b in range(3):
            halo_ref[k, :, b * chans : (b + 1) * chans] = pad_ref[k, 7 + b : 7 + b + WP, :].astype(BF16)
    parts = [jnp.dot(halo_ref[k], v_ref[2 * side, :, lo * chans : hi * chans], preferred_element_type=F32)
             for k, (lo, hi) in enumerate(((2, 3), (1, 3), (0, 2), (0, 1)))]
    total0 = parts[0] + parts[1][:, :chans] + parts[2][:, :chans]
    total1 = parts[1][:, chans:] + parts[2][:, chans:] + parts[3]
    return rim0 + total0[:width], rim1 + total1[:width]


def half_kernel(side, x_ref, left_ref, right_ref, beyond_ref, v_ref, x0_ref, x1_ref, xa0_ref, coef_ref, bias_ref, *refs):
    if side == 0:
        y_ref, new_ref, xa_ref, pad_ref, flat_ref, halo_ref, line_ref = refs
        frame_taps(1, x_ref, left_ref, right_ref, coef_ref[2:3], coef_ref[3:4], pad_ref, flat_ref, new_ref, xa_ref)
    else:
        xa_ref, y_ref, pad_ref, flat_ref, halo_ref, line_ref = refs
    _, width, rows, chans = x_ref.shape
    first, count, rim = (EARLY, rows - EARLY, rows - 1) if side else (0, EARLY, 0)
    total = (product_with(x0_ref, rim, x1_ref, first, count, v_ref, 2)
             + product_with(x1_ref, rim, xa0_ref, first, count, v_ref, 1)
             + product_with(xa0_ref, rim, xa_ref, first, count, v_ref, 0))
    put_lines(flat_ref, x_ref[0].astype(F32).reshape(width * rows, chans))
    rim0 = get_row(flat_ref, rim, rows, width) + bias_ref[...] + total[count * WP : count * WP + width]
    put_lines(flat_ref, x_ref[1].astype(F32).reshape(width * rows, chans))
    rim1 = finish_rows(total, first, count, flat_ref, bias_ref[...], width, rows, line_ref, 0)
    for f, row in enumerate(edge_part(side, beyond_ref, v_ref, coef_ref, rim0, rim1, pad_ref, halo_ref)):
        put_cells(line_ref, count - 1 + f, row)
    y_ref[...] = line_ref[...].astype(BF16)


def spread_kernel(y0_ref, half_ref, new0_ref, new1_ref, flat_ref, new_ref):
    new_ref[0] = new0_ref[...]
    new_ref[1] = new1_ref[...]
    _, width, rows, _ = new_ref.shape
    y0, half = y0_ref[...].astype(F32), half_ref[...].astype(F32)
    for r in range(rows - 2):
        put_row(flat_ref.at[0], r + 1, rows, width, y0[r * width : (r + 1) * width])
    for f in range(2):
        put_row(flat_ref.at[f], 0, rows, width, half[(EARLY - 1 + f) * width : (EARLY + f) * width])
    for at in range(EARLY - 1):
        put_row(flat_ref.at[1], at + 1, rows, width, half[at * width : (at + 1) * width])


def join_kernel(flat_ref, half_ref, out_hbm, scr_ref, out_ref, sems):
    _, width, rows, chans = out_ref.shape
    line = lax.broadcasted_iota(jnp.int32, (width * rows, LANES), 0) & (rows - 1)
    half = half_ref[...].astype(F32)
    late_rows = rows - EARLY
    copies = []
    for f, late in ((0, line == rows - 1), (1, line >= rows - late_rows)):
        put_row(scr_ref.at[f], rows - 1, rows, width, half[(late_rows - 1 + f) * width : (late_rows + f) * width])
        if f == 1:
            for at in range(late_rows - 1):
                put_row(scr_ref.at[1], rows - late_rows + at, rows, width, half[at * width : (at + 1) * width])
        for j in range(flat_ref.shape[1]):
            whole = jnp.where(late, scr_ref[f, j], flat_ref[f, j])
            out_ref[f, :, :, j * LANES : (j + 1) * LANES] = whole.astype(BF16).reshape(width, rows, LANES)
        copies.append(pltpu.make_async_copy(out_ref.at[f], out_hbm.at[f], sems.at[f]))
        copies[-1].start()
    wait_all(copies)


def in_hbm(x):
    return pltpu.with_memory_space_constraint(x, pltpu.HBM)


def on_device(frames_in, cache, kernel, gain, conv_bias):
    x = in_hbm(jnp.transpose(frames_in[0][:, 0], (0, 2, 1, 3)))
    c = in_hbm(jnp.transpose(cache[0][:, 0], (0, 2, 1, 3)))
    frames, width, rows, chans = x.shape
    tiles = lax.axis_size("tile")
    sections = lax.axis_size("section")
    weights = in_hbm(kernel.reshape(3, 3, 3 * chans, chans))
    inner = rows - 2
    sds = jax.ShapeDtypeStruct
    HBM = pl.BlockSpec(memory_space=pltpu.HBM)
    DMA = pltpu.SemaphoreType.DMA

    taps = pltpu.VMEM((rows + 2, WP, 3 * chans), BF16)
    acc = (rows * WP, chans)
    cols = sds((4, rows, chans), F32)
    frame = pltpu.VMEM((width, rows, chans), BF16)
    both = pltpu.VMEM((frames, width, rows, chans), BF16)
    pad = pltpu.VMEM((rows, 80, chans), F32)
    flat = pltpu.VMEM((chans // LANES, width * rows, LANES), F32)
    edge_rows = sds((4, WP, chans), BF16)

    def call(body, name, us, in_specs, out_specs, out_shape, scratch, aliases={}):
        return pl.pallas_call(body, input_output_aliases=aliases, out_shape=out_shape, in_specs=in_specs, out_specs=out_specs,
                              scratch_shapes=scratch, compiler_params=params(), name=name, cost_estimate=cost(us))

    stat, first_col, last_col = call(
        first_kernel, "local_stats", 1, [HBM] * 2, [VMEM] * 3,
        (sds((tiles, 1, 128), F32), sds((4, rows, chans), BF16), sds((4, rows, chans), BF16)),
        [both, pltpu.VMEM((2, 2, rows, chans), BF16), DMA((2, PARTS)), DMA((2, 2))],
    )(x, c)
    stats = lax.all_to_all(stat, "tile", 0, 0, tiled=True)
    next_col = [(i, i - i % TCOL + (i + 1) % TCOL) for i in range(tiles)]
    next_row = [(i, (i + TCOL) % tiles) for i in range(tiles)]
    back = lambda pairs: [(j, i) for i, j in pairs]
    from_left = lax.ppermute(last_col, "tile", next_col)
    from_right = lax.ppermute(first_col, "tile", back(next_col))
    bottom, top, left, right = call(
        rows_kernel, "pack_rows", 2, [HBM, HBM, VMEM, VMEM], [VMEM] * 4, (edge_rows, edge_rows, cols, cols),
        [pltpu.VMEM((4, width, rows, chans), BF16), flat, DMA((4, PARTS))],
    )(c, x, from_left, from_right)
    above = lax.ppermute(bottom, "tile", next_row)
    below = lax.ppermute(top, "tile", back(next_row))
    onward = [(i, (i + 1) % sections) for i in range(sections)]
    y0, new0, v, coef, xv, x0, x1, xa0 = call(
        functools.partial(frame0_kernel, tiles), "frame0", 10, [VMEM, HBM, HBM, VMEM, VMEM, HBM, VMEM, VMEM], [VMEM] * 8,
        (sds((inner * width, chans), BF16), frame, pltpu.VMEM((3, 3 * chans, 3 * chans), BF16),
         pltpu.VMEM((8, chans), F32), both, taps, taps, taps),
        [both, pltpu.VMEM(acc, F32), pad, flat, pltpu.VMEM((inner * width, chans), F32),
         DMA((4, PARTS)), DMA((3, 3))],
    )(stats, c, x, left, right, weights, gain, conv_bias)
    y0 = lax.ppermute(y0, "section", onward)
    early = ((EARLY + 1) * width, chans)
    later = ((rows - EARLY + 1) * width, chans)
    halo = pltpu.VMEM((4, WP, 3 * chans), BF16)
    half_a, new1, xa1 = call(
        functools.partial(half_kernel, 0), "frame1_first", 4, [VMEM] * 10, [VMEM] * 3, (sds(early, BF16), frame, taps),
        [pad, flat, halo, pltpu.VMEM(early, F32)],
    )(xv, left, right, above, v, x0, x1, xa0, coef, conv_bias)
    half_a = lax.ppermute(half_a, "section", onward)
    half_b = call(
        functools.partial(half_kernel, 1), "frame1_second", 4, [VMEM] * 11, VMEM, sds(later, BF16),
        [pad, flat, halo, pltpu.VMEM(later, F32)],
    )(xv, left, right, below, v, x0, x1, xa0, coef, conv_bias, xa1)
    half_b = lax.ppermute(half_b, "section", onward)
    spread, new = call(
        spread_kernel, "spread_rows", 10, [VMEM] * 4, [VMEM] * 2,
        (pltpu.VMEM((frames, chans // LANES, width * rows, LANES), F32), sds((frames, width, rows, chans), BF16)), [],
    )(y0, half_a, new0, new1)
    handed = call(
        join_kernel, "join_rows", 1, [VMEM] * 2, HBM, sds((frames, width, rows, chans), BF16),
        [pltpu.VMEM((frames, chans // LANES, width * rows, LANES), F32), both, DMA((2,))],
    )(spread, half_b)
    handed = jnp.transpose(handed, (0, 2, 1, 3))
    new = jnp.transpose(new, (0, 2, 1, 3))
    return (handed[None, :, None], new[None, :, None])


def solution(mesh):
    tiled = P("section", None, "tile", None, None, None)
    in_specs = (tiled, tiled, P("section", None, None, None, None, None), P("section", None), P("section", None))
    return jax.shard_map(
        on_device, mesh=mesh, in_specs=in_specs, out_specs=(tiled, tiled), check_vma=False
    )
```

```python
import functools

import jax
import jax.numpy as jnp
from jax import lax
from jax.experimental import pallas as pl
from jax.experimental.pallas import tpu as pltpu
from jax.sharding import PartitionSpec as P

GROUPS = 32
TCOL = 4
EPS = 1e-06
WP = 64
F32 = jnp.float32
BF16 = jnp.bfloat16
VMEM = pl.BlockSpec(memory_space=pltpu.VMEM)
ANY = pl.BlockSpec(memory_space=pl.ANY)
LIMIT = 20 * 1024 * 1024


def cost(us):
    return pl.CostEstimate(flops=int(us * 1e9), bytes_accessed=int(us * 3e6), transcendentals=0)


def params():
    return pltpu.CompilerParams(vmem_limit_bytes=LIMIT)


def split3(x):
    high = x.astype(BF16)
    rest = x - high.astype(F32)
    mid = rest.astype(BF16)
    low = (rest - mid.astype(F32)).astype(BF16)
    return high, mid, low


def exact_dot(x, onehot):
    pad = jnp.zeros_like(x)
    parts = split3(x)
    lhs = jnp.concatenate([jnp.concatenate([p.astype(F32), pad], axis=0) for p in parts], axis=0)
    got = jnp.dot(lhs.astype(BF16), onehot, preferred_element_type=F32)
    return got[0:8] + got[16:24] + got[32:40]


def to_group(chans):
    size = chans // GROUPS
    chan = lax.broadcasted_iota(jnp.int32, (chans, 128), 0)
    first = (lax.broadcasted_iota(jnp.int32, (chans, 128), 1) & (GROUPS - 1)) * size
    return jnp.where((chan >= first) & (chan < first + size), 1.0, 0.0).astype(BF16)


def same_group(chans):
    size = chans // GROUPS
    row = lax.broadcasted_iota(jnp.int32, (chans, 1), 0)
    col = lax.broadcasted_iota(jnp.int32, (1, chans), 1)
    of = lambda c: (c * ((1 << 18) // size + 1)) >> 18
    return jnp.where(of(row) == of(col), 1.0, 0.0).astype(BF16)


def from_group(chans, block):
    size = chans // GROUPS
    lane = lax.broadcasted_iota(jnp.int32, (128, chans), 0)
    chan = lax.broadcasted_iota(jnp.int32, (128, chans), 1)
    first = (lane & (GROUPS - 1)) * size
    hit = (chan >= first) & (chan < first + size) & ((lane >> 5) == block)
    return jnp.where(hit, 1.0, 0.0).astype(BF16)


PARTS = 12


def fetch(hbm_ref, f, vmem_ref, sems):
    parts = sems.shape[0]
    step = hbm_ref.shape[1] // parts
    copies = [pltpu.make_async_copy(hbm_ref.at[f, pl.ds(p * step, step)], vmem_ref.at[pl.ds(p * step, step)],
                                    sems.at[p]) for p in range(parts)]
    for copy in copies:
        copy.start()
    return copies


def wait_all(copies):
    for copy in copies:
        copy.wait()


def first_kernel(x_hbm, c_hbm, stat_ref, first_ref, last_ref, x_ref, edge_ref, sems, edge_sems):
    frames, width, rows, chans = x_ref.shape
    loads = [fetch(x_hbm, f, x_ref.at[f], sems.at[f]) for f in range(frames)]
    edges = []
    for f in range(2):
        for at, w in ((0, 0), (1, width - 1)):
            edges.append(pltpu.make_async_copy(c_hbm.at[f, w], edge_ref.at[f, at], edge_sems.at[f, at]))
    for copy in edges:
        copy.start()
    size = chans // GROUPS
    count = rows * width
    every, same = to_group(chans), same_group(chans)
    sums, squares = [], []
    for f in range(frames):
        wait_all(loads[f])
        x = x_ref[f].astype(F32)
        total = jnp.sum(jnp.sum(x, axis=0), axis=0, keepdims=True)
        dev = x - (total * (1.0 / count))[None]
        sums.append(total)
        squares.append(jnp.sum(jnp.sum(dev * dev, axis=0), axis=0, keepdims=True))
    wait_all(edges)
    for k in range(4):
        first_ref[k] = edge_ref[k, 0] if k < 2 else x_ref[k - 2, 0]
        last_ref[k] = edge_ref[k, 1] if k < 2 else x_ref[k - 2, width - 1]
    zero = jnp.zeros((1, chans), F32)
    both = jnp.concatenate(sums + [zero] * 6, axis=0)
    spread = exact_dot(both, same)
    off = both * (1.0 / count) - spread * (1.0 / (count * size))
    square = jnp.concatenate(squares + [zero] * 6, axis=0) + count * off * off
    row = lax.broadcasted_iota(jnp.int32, (8, 128), 0)
    lane = lax.broadcasted_iota(jnp.int32, (8, 128), 1)
    mix_sum = exact_dot(both, every)
    mix_square = exact_dot(square, every)
    kind = lane >> 5
    mixed = jnp.where((row == 0) & (kind == 0), mix_sum, 0.0)
    mixed = mixed + jnp.where((row == 1) & (kind == 2), mix_sum, 0.0)
    mixed = mixed + jnp.where((row == 0) & (kind == 1), mix_square, 0.0)
    mixed = mixed + jnp.where((row == 1) & (kind == 3), mix_square, 0.0)
    line = jnp.sum(mixed, axis=0, keepdims=True)
    stat_ref[...] = jnp.broadcast_to(line[None], stat_ref.shape)


LANES = 128


def put_lines(flat_ref, lines):
    for j in range(flat_ref.shape[0]):
        flat_ref[j] = lines[:, j * LANES : (j + 1) * LANES]


def get_row(flat_ref, r, rows, width):
    return jnp.concatenate(
        [flat_ref[j, pl.ds(r, width, stride=rows), :] for j in range(flat_ref.shape[0])], axis=1)


def put_row(flat_ref, r, rows, width, value):
    for j in range(flat_ref.shape[0]):
        flat_ref[j, pl.ds(r, width, stride=rows), :] = value[:, j * LANES : (j + 1) * LANES]


def build_taps(flat_ref, left, right, pad_ref, out_ref, rows, width):
    chans = pad_ref.shape[-1]
    for r in range(rows):
        pad_ref[r, 8 : 8 + width, :] = get_row(flat_ref, r, rows, width)
        pad_ref[r, 7:8, :] = left[r : r + 1]
        pad_ref[r, 8 + width : 9 + width, :] = right[r : r + 1]
    for b in range(3):
        out_ref[1 : 1 + rows, :, b * chans : (b + 1) * chans] = pad_ref[:, 7 + b : 7 + b + WP, :].astype(BF16)
    out_ref[0] = jnp.zeros_like(out_ref[0])
    out_ref[rows + 1] = jnp.zeros_like(out_ref[0])


def clear_tail(pad_ref, width):
    pad_ref[:, 8 + width :, :] = jnp.zeros_like(pad_ref[:, 8 + width :, :])


def tile_place():
    tile = lax.axis_index("tile")
    return lax.div(tile, TCOL), lax.rem(tile, TCOL)


EARLY = 5


def wide_taps(taps_ref, first, count):
    return jnp.concatenate([taps_ref[first + a : first + a + count].reshape(count * WP, -1) for a in range(3)], axis=1)


def product(taps_ref, first, count, v_ref, at):
    return jnp.dot(wide_taps(taps_ref, first, count), tap_weights(v_ref, at, at + 1), preferred_element_type=F32)


def product_with(rim_taps_ref, rim, taps_ref, first, count, v_ref, at):
    lhs = jnp.concatenate([wide_taps(taps_ref, first, count), wide_taps(rim_taps_ref, rim, 1)], axis=0)
    return jnp.dot(lhs, tap_weights(v_ref, at, at + 1), preferred_element_type=F32)


def tap_weights(v_ref, lo, hi):
    chans = v_ref.shape[1] // 3
    return v_ref[:, :, lo * chans : hi * chans].reshape(9 * chans, (hi - lo) * chans)


def rows_kernel(c_hbm, x_hbm, from_left_ref, from_right_ref, bottom_ref, top_ref, left_ref, right_ref,
                frame_ref, flat_ref, sems):
    _, width, rows, chans = frame_ref.shape
    loads = [fetch(c_hbm if k < 2 else x_hbm, k % 2, frame_ref.at[k], sems.at[k]) for k in range(4)]
    _, col = tile_place()
    left_ref[...] = jnp.where(col > 0, from_left_ref[...].astype(F32), 0.0)
    right_ref[...] = jnp.where(col < TCOL - 1, from_right_ref[...].astype(F32), 0.0)
    for k in range(4):
        wait_all(loads[k])
        put_lines(flat_ref, frame_ref[k].astype(F32).reshape(width * rows, chans))
        for out_ref, r in ((bottom_ref, rows - 1), (top_ref, 0)):
            last = jnp.concatenate([left_ref[k, r : r + 1], right_ref[k, r : r + 1],
                                    jnp.zeros((WP - width - 2, chans), F32)], axis=0)
            line = jnp.concatenate([get_row(flat_ref, r, rows, width), last], axis=0)
            out_ref[k] = line.astype(BF16)


def silu(v):
    return v / (1.0 + jnp.exp(-v))


def activated(x, scale, shift):
    return silu(x * scale + shift)


def frame_taps(f, x_ref, left_ref, right_ref, scale, shift, pad_ref, flat_ref, new_ref, out_ref):
    _, width, rows, chans = x_ref.shape
    _, col = tile_place()
    act = activated(x_ref[f].astype(F32).reshape(width * rows, chans), scale, shift)
    put_lines(flat_ref, act)
    new_ref[...] = act.astype(BF16).reshape(width, rows, chans)
    left = activated(left_ref[2 + f], scale, shift)
    right = activated(right_ref[2 + f], scale, shift)
    left = jnp.where(col > 0, left, 0.0)
    right = jnp.where(col < TCOL - 1, right, 0.0)
    clear_tail(pad_ref, width)
    build_taps(flat_ref, left, right, pad_ref, out_ref, rows, width)


def put_cells(line_ref, at, value):
    line_ref[at * value.shape[0] : (at + 1) * value.shape[0], :] = value


def finish_rows(total, first, count, flat_ref, bias, width, rows, line_ref, at_line):
    rim = None
    for at in range(count):
        r = first + at
        whole = get_row(flat_ref, r, rows, width) + bias + total[at * WP : at * WP + width]
        if r in (0, rows - 1):
            rim = whole
        else:
            put_cells(line_ref, at_line, whole)
            at_line += 1
    return rim


def frame0_kernel(tiles, stat_ref, c_hbm, x_hbm, left_ref, right_ref, w_hbm, gain_ref, bias_ref,
                  y_ref, new_ref, v_ref, coef_ref, x_ref, x0_ref, x1_ref, xa_ref,
                  c_ref, sum_ref, pad_ref, flat_ref, line_ref, frame_sems, sems):
    _, width, rows, chans = x_ref.shape
    loads = [fetch(c_hbm, 0, c_ref.at[0], frame_sems.at[0]), fetch(c_hbm, 1, c_ref.at[1], frame_sems.at[1]),
             fetch(x_hbm, 0, x_ref.at[0], frame_sems.at[2])]
    copies = {}
    for t in range(3):
        for a in range(3):
            copies[t, a] = pltpu.make_async_copy(
                w_hbm.at[t, a], v_ref.at[a, :, (2 - t) * chans : (3 - t) * chans], sems.at[t, a])
            copies[t, a].start()

    def wait_weights(t):
        for a in range(3):
            copies[t, a].wait()

    loads.append(fetch(x_hbm, 1, x_ref.at[1], frame_sems.at[3]))
    part = rows * width * (chans // GROUPS)
    count = part * tiles
    stat = stat_ref[...].reshape(tiles, 128)
    moved = pltpu.roll(stat, GROUPS, 1)
    mean = jnp.sum(stat, axis=0, keepdims=True) * (1.0 / count)
    mean_moved = jnp.sum(moved, axis=0, keepdims=True) * (1.0 / count)
    off = moved * (1.0 / part) - mean_moved
    var = jnp.sum(stat + part * off * off, axis=0, keepdims=True) * (1.0 / count)
    lane = lax.broadcasted_iota(jnp.int32, (1, 128), 1)
    is_mean = ((lane >> 5) & 1) == 0
    both = jnp.where(is_mean, mean, lax.rsqrt(jnp.maximum(var, 0.0) + EPS))
    both = jnp.broadcast_to(both, (8, 128))
    gain = gain_ref[...]
    for f in range(2):
        means = exact_dot(both, from_group(chans, 2 * f))[0:1]
        rstds = exact_dot(both, from_group(chans, 2 * f + 1))[0:1]
        scale = rstds * gain
        coef_ref[2 * f : 2 * f + 1, :] = scale
        coef_ref[2 * f + 1 : 2 * f + 2, :] = -means * scale
    clear_tail(pad_ref, width)
    for k, out_ref in ((0, x0_ref), (1, x1_ref)):
        wait_all(loads[k])
        put_lines(flat_ref, c_ref[k].astype(F32).reshape(width * rows, chans))
        build_taps(flat_ref, left_ref[k], right_ref[k], pad_ref, out_ref, rows, width)
    wait_all(loads[2])
    frame_taps(0, x_ref, left_ref, right_ref, coef_ref[0:1], coef_ref[1:2], pad_ref, flat_ref, new_ref, xa_ref)
    put_lines(flat_ref, x_ref[0].astype(F32).reshape(width * rows, chans))
    step = (rows - 2) // 2
    firsts = (1, 1 + step)
    wait_weights(0)
    for first in firsts:
        sum_ref[first * WP : (first + step) * WP] = product(x0_ref, first, step, v_ref, 2)
    wait_weights(1)
    for first in firsts:
        sum_ref[first * WP : (first + step) * WP] += product(x1_ref, first, step, v_ref, 1)
    wait_weights(2)
    for first in firsts:
        total = sum_ref[first * WP : (first + step) * WP] + product(xa_ref, first, step, v_ref, 0)
        finish_rows(total, first, step, flat_ref, bias_ref[...], width, rows, line_ref, first - 1)
    y_ref[...] = line_ref[...].astype(BF16)
    wait_all(loads[3])


def edge_part(side, src_ref, v_ref, coef_ref, rim0, rim1, pad_ref, halo_ref):
    width, chans = rim0.shape
    row, col = tile_place()
    last = lax.div(lax.axis_size("tile"), TCOL) - 1
    inside = (row > 0) if side == 0 else (row < last)
    clear_tail(pad_ref, width)
    for k in range(4):
        cells = src_ref[k].astype(F32)
        if k >= 2:
            f = k - 2
            cells = activated(cells, coef_ref[2 * f : 2 * f + 1], coef_ref[2 * f + 1 : 2 * f + 2])
        at = lax.broadcasted_iota(jnp.int32, cells.shape, 0)
        keep = (at < width) | ((at == width) & (col > 0)) | ((at == width + 1) & (col < TCOL - 1))
        cells = jnp.where(keep & inside, cells, 0.0)
        pad_ref[k, 8 : 8 + width, :] = cells[0:width]
        pad_ref[k, 7:8, :] = cells[width : width + 1]
        pad_ref[k, 8 + width : 9 + width, :] = cells[width + 1 : width + 2]
        for b in range(3):
            halo_ref[k, :, b * chans : (b + 1) * chans] = pad_ref[k, 7 + b : 7 + b + WP, :].astype(BF16)
    parts = [jnp.dot(halo_ref[k], v_ref[2 * side, :, lo * chans : hi * chans], preferred_element_type=F32)
             for k, (lo, hi) in enumerate(((2, 3), (1, 3), (0, 2), (0, 1)))]
    total0 = parts[0] + parts[1][:, :chans] + parts[2][:, :chans]
    total1 = parts[1][:, chans:] + parts[2][:, chans:] + parts[3]
    return rim0 + total0[:width], rim1 + total1[:width]


def half_kernel(side, x_ref, left_ref, right_ref, beyond_ref, v_ref, x0_ref, x1_ref, xa0_ref, coef_ref, bias_ref, *refs):
    if side == 0:
        y_ref, new_ref, xa_ref, pad_ref, flat_ref, halo_ref, line_ref = refs
        frame_taps(1, x_ref, left_ref, right_ref, coef_ref[2:3], coef_ref[3:4], pad_ref, flat_ref, new_ref, xa_ref)
    else:
        xa_ref, y_ref, pad_ref, flat_ref, halo_ref, line_ref = refs
    _, width, rows, chans = x_ref.shape
    first, count, rim = (EARLY, rows - EARLY, rows - 1) if side else (0, EARLY, 0)
    total = (product_with(x0_ref, rim, x1_ref, first, count, v_ref, 2)
             + product_with(x1_ref, rim, xa0_ref, first, count, v_ref, 1)
             + product_with(xa0_ref, rim, xa_ref, first, count, v_ref, 0))
    put_lines(flat_ref, x_ref[0].astype(F32).reshape(width * rows, chans))
    rim0 = get_row(flat_ref, rim, rows, width) + bias_ref[...] + total[count * WP : count * WP + width]
    put_lines(flat_ref, x_ref[1].astype(F32).reshape(width * rows, chans))
    rim1 = finish_rows(total, first, count, flat_ref, bias_ref[...], width, rows, line_ref, 0)
    for f, row in enumerate(edge_part(side, beyond_ref, v_ref, coef_ref, rim0, rim1, pad_ref, halo_ref)):
        put_cells(line_ref, count - 1 + f, row)
    y_ref[...] = line_ref[...].astype(BF16)


def spread_kernel(y0_ref, half_ref, new0_ref, new1_ref, flat_ref, new_ref):
    new_ref[0] = new0_ref[...]
    new_ref[1] = new1_ref[...]
    _, width, rows, _ = new_ref.shape
    y0, half = y0_ref[...].astype(F32), half_ref[...].astype(F32)
    for r in range(rows - 2):
        put_row(flat_ref.at[0], r + 1, rows, width, y0[r * width : (r + 1) * width])
    for f in range(2):
        put_row(flat_ref.at[f], 0, rows, width, half[(EARLY - 1 + f) * width : (EARLY + f) * width])
    for at in range(EARLY - 1):
        put_row(flat_ref.at[1], at + 1, rows, width, half[at * width : (at + 1) * width])


def join_kernel(flat_ref, half_ref, out_hbm, scr_ref, out_ref, sems):
    _, width, rows, chans = out_ref.shape
    line = lax.broadcasted_iota(jnp.int32, (width * rows, LANES), 0) & (rows - 1)
    half = half_ref[...].astype(F32)
    late_rows = rows - EARLY
    copies = []
    for f, late in ((0, line == rows - 1), (1, line >= rows - late_rows)):
        put_row(scr_ref.at[f], rows - 1, rows, width, half[(late_rows - 1 + f) * width : (late_rows + f) * width])
        if f == 1:
            for at in range(late_rows - 1):
                put_row(scr_ref.at[1], rows - late_rows + at, rows, width, half[at * width : (at + 1) * width])
        for j in range(flat_ref.shape[1]):
            whole = jnp.where(late, scr_ref[f, j], flat_ref[f, j])
            out_ref[f, :, :, j * LANES : (j + 1) * LANES] = whole.astype(BF16).reshape(width, rows, LANES)
        copies.append(pltpu.make_async_copy(out_ref.at[f], out_hbm.at[f], sems.at[f]))
        copies[-1].start()
    wait_all(copies)


def in_hbm(x):
    return pltpu.with_memory_space_constraint(x, pltpu.HBM)


def on_device(frames_in, cache, kernel, gain, conv_bias):
    x = in_hbm(jnp.transpose(frames_in[0][:, 0], (0, 2, 1, 3)))
    c = in_hbm(jnp.transpose(cache[0][:, 0], (0, 2, 1, 3)))
    frames, width, rows, chans = x.shape
    tiles = lax.axis_size("tile")
    sections = lax.axis_size("section")
    weights = in_hbm(kernel.reshape(3, 3, 3 * chans, chans))
    inner = rows - 2
    sds = jax.ShapeDtypeStruct
    HBM = pl.BlockSpec(memory_space=pltpu.HBM)
    DMA = pltpu.SemaphoreType.DMA

    taps = pltpu.VMEM((rows + 2, WP, 3 * chans), BF16)
    acc = (rows * WP, chans)
    cols = sds((4, rows, chans), F32)
    frame = pltpu.VMEM((width, rows, chans), BF16)
    both = pltpu.VMEM((frames, width, rows, chans), BF16)
    pad = pltpu.VMEM((rows, 80, chans), F32)
    flat = pltpu.VMEM((chans // LANES, width * rows, LANES), F32)
    edge_rows = sds((4, WP, chans), BF16)

    def call(body, name, us, in_specs, out_specs, out_shape, scratch, aliases={}):
        return pl.pallas_call(body, input_output_aliases=aliases, out_shape=out_shape, in_specs=in_specs, out_specs=out_specs,
                              scratch_shapes=scratch, compiler_params=params(), name=name, cost_estimate=cost(us))

    stat, first_col, last_col = call(
        first_kernel, "local_stats", 1, [HBM] * 2, [VMEM] * 3,
        (sds((tiles, 1, 128), F32), sds((4, rows, chans), BF16), sds((4, rows, chans), BF16)),
        [both, pltpu.VMEM((2, 2, rows, chans), BF16), DMA((2, 1)), DMA((2, 2))],
    )(x, c)
    stats = lax.all_to_all(stat, "tile", 0, 0, tiled=True)
    next_col = [(i, i - i % TCOL + (i + 1) % TCOL) for i in range(tiles)]
    next_row = [(i, (i + TCOL) % tiles) for i in range(tiles)]
    back = lambda pairs: [(j, i) for i, j in pairs]
    from_left = lax.ppermute(last_col, "tile", next_col)
    from_right = lax.ppermute(first_col, "tile", back(next_col))
    bottom, top, left, right = call(
        rows_kernel, "pack_rows", 2, [HBM, HBM, VMEM, VMEM], [VMEM] * 4, (edge_rows, edge_rows, cols, cols),
        [pltpu.VMEM((4, width, rows, chans), BF16), flat, DMA((4, 1))],
    )(c, x, from_left, from_right)
    above = lax.ppermute(bottom, "tile", next_row)
    below = lax.ppermute(top, "tile", back(next_row))
    onward = [(i, (i + 1) % sections) for i in range(sections)]
    y0, new0, v, coef, xv, x0, x1, xa0 = call(
        functools.partial(frame0_kernel, tiles), "frame0", 10, [VMEM, HBM, HBM, VMEM, VMEM, HBM, VMEM, VMEM], [VMEM] * 8,
        (sds((inner * width, chans), BF16), frame, pltpu.VMEM((3, 3 * chans, 3 * chans), BF16),
         pltpu.VMEM((8, chans), F32), both, taps, taps, taps),
        [both, pltpu.VMEM(acc, F32), pad, flat, pltpu.VMEM((inner * width, chans), F32),
         DMA((4, PARTS)), DMA((3, 3))],
    )(stats, c, x, left, right, weights, gain, conv_bias)
    y0 = lax.ppermute(y0, "section", onward)
    early = ((EARLY + 1) * width, chans)
    later = ((rows - EARLY + 1) * width, chans)
    halo = pltpu.VMEM((4, WP, 3 * chans), BF16)
    half_a, new1, xa1 = call(
        functools.partial(half_kernel, 0), "frame1_first", 4, [VMEM] * 10, [VMEM] * 3, (sds(early, BF16), frame, taps),
        [pad, flat, halo, pltpu.VMEM(early, F32)],
    )(xv, left, right, above, v, x0, x1, xa0, coef, conv_bias)
    half_a = lax.ppermute(half_a, "section", onward)
    half_b = call(
        functools.partial(half_kernel, 1), "frame1_second", 4, [VMEM] * 11, VMEM, sds(later, BF16),
        [pad, flat, halo, pltpu.VMEM(later, F32)],
    )(xv, left, right, below, v, x0, x1, xa0, coef, conv_bias, xa1)
    half_b = lax.ppermute(half_b, "section", onward)
    spread, new = call(
        spread_kernel, "spread_rows", 10, [VMEM] * 4, [VMEM] * 2,
        (pltpu.VMEM((frames, chans // LANES, width * rows, LANES), F32), sds((frames, width, rows, chans), BF16)), [],
    )(y0, half_a, new0, new1)
    handed = call(
        join_kernel, "join_rows", 1, [VMEM] * 2, HBM, sds((frames, width, rows, chans), BF16),
        [pltpu.VMEM((frames, chans // LANES, width * rows, LANES), F32), both, DMA((2,))],
    )(spread, half_b)
    handed = jnp.transpose(handed, (0, 2, 1, 3))
    new = jnp.transpose(new, (0, 2, 1, 3))
    return (handed[None, :, None], new[None, :, None])


def solution(mesh):
    tiled = P("section", None, "tile", None, None, None)
    in_specs = (tiled, tiled, P("section", None, None, None, None, None), P("section", None), P("section", None))
    return jax.shard_map(
        on_device, mesh=mesh, in_specs=in_specs, out_specs=(tiled, tiled), check_vma=False
    )
```
